256 devices in a mesh: ctx: 8 (over z_hi, x), exp: 32 (over y, z_lo, core).
Axes of the slice: x: 4, y: 4, z: 8 (z_hi: 2, z_lo: 4; z = z_hi * 4 + z_lo), core: 2. Of those that a mesh axis runs over, the one named last changes fastest.
Arguments:
- queries: bfloat16 [32, 1024, 2048], P('exp', 'ctx'), may hold values from -8 to 8
- key_rows: bfloat16 [32, 1024, 256], P('exp', 'ctx'), may hold values from -8 to 8
- value_rows: bfloat16 [32, 1024, 256], P('exp', 'ctx'), may hold values from -6 to 6
- out_grad: bfloat16 [32, 1024, 2048], P('exp', 'ctx'), may hold values from -6 to 6
- tokens: bfloat16 [32, 1024, 2880], P('exp', 'ctx'), may hold values from -6 to 6
- token_grad: bfloat16 [32, 1024, 2880], P('exp', 'ctx'), may hold values from -6 to 6
- route_ids: int32 [32, 1024, 4], P('exp', 'ctx'), may hold values from 0 to 127, as said below
- route_probs: float32 [32, 1024, 4], P('exp', 'ctx'), may hold values from 0.05 to 1
- entry_weight: bfloat16 [32, 2880, 2, 1440], P('exp', None, None, 'ctx'), may hold values from -0.109375 to 0.109375
- exit_weight: bfloat16 [32, 1440, 2880], P('exp', 'ctx'), may hold values from -0.15625 to 0.15625
Outputs:
- query_grad: bfloat16 [32, 1024, 2048], P('exp', 'ctx')
- key_grad: bfloat16 [32, 1024, 256], P('exp', 'ctx')
- value_grad: bfloat16 [32, 1024, 256], P('exp', 'ctx')
- input_grad: bfloat16 [32, 1024, 2880], P('exp', 'ctx')
- entry_grad: bfloat16 [32, 2880, 2, 1440], P('exp', None, None, 'ctx')
- exit_grad: bfloat16 [32, 1440, 2880], P('exp', 'ctx')
The draws below stay inside these ranges and needn't reach their ends.
Inputs may be any that keep to these rules, and one draw needn't show every extreme that they name: `route_ids`: each token names 4 different experts. Tokens form aligned blocks of 128 positions in order (sequence by sequence); within one block no expert is named more than 5 times, and in every draw one expert below 32 is named exactly 5 times in every block.
All inputs are finite; a program needn't handle non-finite values.
Results may differ from the reference program's by a relative error of at most 0.017.
Values may be sent and summed in bfloat16 or wider, within the bound.
A program may use at most 192 MiB of HBM per device.

```python
import math
import jax
import jax.numpy as jnp
from jax import lax

D = 2880
HID = 1440
QH = 32
KH = 4
HEAD = 64
EXPERTS = 128
TOP = 4
TOK_DEV = 128
EXP_WIN = 32
SEQS = 32
SEQ = 1024
CAP = 5
N_CTX = 8


def draw_queries(key, part):
    key = jax.random.fold_in(key, 5)
    array_shape = (SEQS, SEQ, QH * HEAD)
    drawn = jnp.clip(jax.random.normal(key, array_shape, jnp.float32), -8.0, 8.0)
    return drawn.astype(jnp.bfloat16)


def draw_key_rows(key, part):
    key = jax.random.fold_in(key, 6)
    array_shape = (SEQS, SEQ, KH * HEAD)
    drawn = jnp.clip(jax.random.normal(key, array_shape, jnp.float32), -8.0, 8.0)
    return drawn.astype(jnp.bfloat16)


def draw_route_ids(key, part):
    key = jax.random.fold_in(key, 7)
    busiest = jax.random.randint(jax.random.fold_in(key, 1), (), 0, EXP_WIN)
    block_count = SEQS * SEQ // TOK_DEV

    def one_block(block_index):
        block_key = jax.random.fold_in(key, block_index + 2)
        ranking = jax.random.permutation(jax.random.fold_in(block_key, 0), EXPERTS)
        where_busiest = jnp.argmax(ranking == busiest)
        leading = ranking[0]
        ranking = ranking.at[where_busiest].set(leading).at[0].set(busiest)
        repeats = jax.random.randint(jax.random.fold_in(block_key, 1), (EXPERTS,), CAP - 1, CAP + 1)
        repeats = repeats.at[0].set(CAP)
        listed = jnp.repeat(ranking, repeats, total_repeat_length=TOK_DEV * TOP)
        routing = listed.reshape(TOP, TOK_DEV).T
        shuffle = jax.random.permutation(jax.random.fold_in(block_key, 2), TOK_DEV)
        return routing[shuffle]
    tables = jax.lax.map(one_block, jnp.arange(block_count))
    return tables.reshape(SEQS, SEQ, TOP).astype(jnp.int32)


def levels(own_key, extent, split, smallest, largest):
    level = 1.0
    for axis_at, parts in split:
        heights = jax.random.uniform(jax.random.fold_in(jax.random.fold_in(own_key, 6), axis_at), (parts,), jnp.float32, smallest / len(split), largest / len(split))
        level = level * jnp.repeat(jnp.exp(heights), extent[axis_at] // parts).reshape((-1,) + (1,) * (len(extent) - 1 - axis_at))
    return level


def bell_draw(stream_key, dims, deviation, reach, shards=(), kind=jnp.bfloat16):
    factor_of = levels(stream_key, dims, shards, -0.22, 0.18) if shards else 1.0
    entries = jax.random.normal(stream_key, dims, jnp.float32) * deviation * factor_of
    return jnp.minimum(jnp.maximum(entries, -reach), reach).astype(kind)


def setup_inputs(seed: int = 0) -> dict:
    arg_keys = jax.random.split(jax.random.key(seed), 11)
    queries = draw_queries(jax.random.fold_in(arg_keys[10], 71), 0)
    key_rows = draw_key_rows(jax.random.fold_in(arg_keys[10], 71), 0)
    value_rows = bell_draw(arg_keys[2], (SEQS, SEQ, KH * HEAD), 1.0, 6.0, ((0, 32), (1, 8)))
    out_grad = bell_draw(arg_keys[3], (SEQS, SEQ, QH * HEAD), 1.0, 6.0, ((0, 32), (1, 8)))
    tokens = bell_draw(arg_keys[4], (SEQS, SEQ, D), 1.0, 6.0, ((0, 32), (1, 8)))
    token_grad = bell_draw(arg_keys[5], (SEQS, SEQ, D), 1.0, 6.0, ((0, 32), (1, 8)))
    route_ids = draw_route_ids(jax.random.fold_in(arg_keys[10], 71), 0)
    route_probs = jnp.clip(jnp.exp(math.log(1.0) - 2.9957323 * jax.random.uniform(arg_keys[7], (SEQS, SEQ, TOP), jnp.float32) ** levels(arg_keys[7], (SEQS, SEQ, TOP), ((0, 32), (1, 8)), -0.2, 0.2)), 0.05, 1.0)
    entry_weight = bell_draw(arg_keys[8], (EXP_WIN, D, 2, HID), D ** -0.5, 0.109375, ((0, 32), (3, 8)))
    exit_weight = bell_draw(arg_keys[9], (EXP_WIN, HID, D), HID ** -0.5, 0.15625, ((0, 32), (1, 8)))
    return {"queries": queries, "key_rows": key_rows, "value_rows": value_rows, "out_grad": out_grad, "tokens": tokens, "token_grad": token_grad, "route_ids": route_ids, "route_probs": route_probs, "entry_weight": entry_weight, "exit_weight": exit_weight}


def widen(array):
    return lax.optimization_barrier(array.astype(jnp.bfloat16)).astype(jnp.float32)


def attention_sequence(operands):
    query_seq, key_seq, value_seq, grad_seq = operands
    length = query_seq.shape[0]
    group_size = QH // KH
    query_heads = query_seq.astype(jnp.float32).reshape(length, KH, group_size, HEAD)
    grad_heads = grad_seq.astype(jnp.float32).reshape(length, KH, group_size, HEAD)
    key_heads = key_seq.astype(jnp.float32).reshape(length, KH, HEAD)
    value_heads = value_seq.astype(jnp.float32).reshape(length, KH, HEAD)
    highest = lax.Precision.HIGHEST
    scores = jnp.einsum("ihgd,jhd->hgij", query_heads, key_heads, precision=highest) * 0.125
    positions = jnp.arange(length)
    causal = positions[None, :] <= positions[:, None]
    row_max = jnp.max(jnp.where(causal, scores, -1e30), axis=-1)
    row_sum = jnp.sum(jnp.where(causal, jnp.exp(scores - row_max[..., None]), 0.0), axis=-1)
    logsum = row_max + jnp.log(row_sum)
    weights = jnp.where(causal, jnp.exp(scores - logsum[..., None]), 0.0)
    prob_grad = jnp.einsum("ihgd,jhd->hgij", grad_heads, value_heads, precision=highest)
    delta = jnp.sum(weights * prob_grad, axis=-1)
    value_grad = jnp.einsum("hgij,ihgd->jhd", widen(weights), grad_heads, precision=highest)
    score_grad = widen(weights * (prob_grad - delta[..., None]))
    query_grad = jnp.einsum("hgij,jhd->ihgd", score_grad, key_heads, precision=highest) * 0.125
    key_grad = jnp.einsum("hgij,ihgd->jhd", score_grad, query_heads, precision=highest) * 0.125
    return (query_grad.reshape(length, -1).astype(jnp.bfloat16),
            key_grad.reshape(length, -1).astype(jnp.bfloat16),
            value_grad.reshape(length, -1).astype(jnp.bfloat16))


def reference(queries, key_rows, value_rows, out_grad, tokens, token_grad, route_ids, route_probs, entry_weight, exit_weight):
    query_grad, key_grad, value_grad = lax.map(attention_sequence, (queries, key_rows, value_rows, out_grad))
    flat_tokens = tokens.reshape(-1, D)
    flat_grads = token_grad.reshape(-1, D)
    flat_ids = route_ids.reshape(-1, TOP)
    flat_probs = route_probs.reshape(-1, TOP)
    rows_total = N_CTX * EXP_WIN * CAP
    slice_width = HID // N_CTX

    def one_expert(carried, operands):
        expert, entry_one, exit_one = operands
        matched = flat_ids == expert
        member = jnp.any(matched, axis=1)
        token_share = jnp.sum(jnp.where(matched, flat_probs, 0.0), axis=1)
        picked = jnp.nonzero(member, size=rows_total, fill_value=0)[0].astype(jnp.int32)
        valid = jnp.arange(rows_total) < jnp.sum(member.astype(jnp.int32))
        rows_in = flat_tokens[picked]
        share_rows = jnp.where(valid, token_share[picked], 0.0)
        grads_in = (flat_grads[picked].astype(jnp.float32) * share_rows[:, None]).astype(jnp.bfloat16)
        entry_flat = entry_one.reshape(D, 2 * HID)
        projected = jnp.dot(rows_in, entry_flat, preferred_element_type=jnp.float32)
        gate = projected[:, :HID]
        upward = projected[:, HID:]
        sigma = jax.nn.sigmoid(gate)
        swish = gate * sigma
        activation = (swish * upward).astype(jnp.bfloat16)
        act_grad = jnp.dot(grads_in, exit_one.T, preferred_element_type=jnp.float32)
        slope = sigma * (1.0 + gate * (1.0 - sigma))
        score_rows = jnp.concatenate([act_grad * upward * slope, act_grad * swish], axis=1).astype(jnp.bfloat16)
        entry_sum = jnp.dot(rows_in.T, score_rows, preferred_element_type=jnp.float32)
        exit_sum = jnp.dot(activation.T, grads_in, preferred_element_type=jnp.float32)
        score_split = score_rows.reshape(rows_total, 2, N_CTX, slice_width)
        entry_split = entry_one.reshape(D, 2, N_CTX, slice_width)
        total = jnp.zeros((rows_total, D), jnp.float32)
        for piece in range(N_CTX):
            left = score_split[:, :, piece, :].reshape(rows_total, 2 * slice_width)
            right = entry_split[:, :, piece, :].reshape(D, 2 * slice_width)
            part_sum = jnp.dot(left, right.T, preferred_element_type=jnp.float32)
            total = total + part_sum.astype(jnp.bfloat16).astype(jnp.float32)
        row_grad = total.astype(jnp.bfloat16).astype(jnp.float32)
        carried = carried.at[picked].add(jnp.where(valid[:, None], row_grad, 0.0))
        return carried, (entry_sum.astype(jnp.bfloat16).reshape(D, 2, HID), exit_sum.astype(jnp.bfloat16))

    start = jnp.zeros((flat_tokens.shape[0], D), jnp.float32)
    expert_numbers = jnp.arange(EXP_WIN).astype(jnp.int32)
    summed, (entry_grad, exit_grad) = lax.scan(one_expert, start, (expert_numbers, entry_weight, exit_weight))
    input_grad = summed.astype(jnp.bfloat16).reshape(SEQS, SEQ, D)
    return (query_grad, key_grad, value_grad, input_grad, entry_grad, exit_grad)
```

```python
import functools

import jax
import jax.numpy as jnp
import numpy as np
from jax import lax
from jax.experimental import pallas as pl
from jax.experimental.pallas import tpu as pltpu
from jax.sharding import PartitionSpec as P

HEAD = 64
CAP = 5
TOK = 128
WIDTH = 2880
FOLD = 1920
BACK = 1024
PAD = 192
EXPERTS = 32
MESH = pl.DeviceIdType.MESH
MIB = 1024 * 1024
SCALE = 0.125
EXP_SCALE = 0.125 * 1.4426950408889634


def nt(a, b):
    return lax.dot_general(a, b, (((1,), (1,)), ((), ())), preferred_element_type=jnp.float32)


def tn(a, b):
    return lax.dot_general(a, b, (((0,), (0,)), ((), ())), preferred_element_type=jnp.float32)


def nn(a, b):
    return lax.dot_general(a, b, (((1,), (0,)), ((), ())), preferred_element_type=jnp.float32)


def attention_body(c, q_ref, g_ref, kv_ref, dq_ref, dkv_ref, s_ref, p_ref, kz_ref, vz_ref, q4, g4, dk2, dv2, dq4):
    length = q_ref.shape[0]
    lane = lax.broadcasted_iota(jnp.int32, (length, 128), 1)
    low = lane < HEAD
    krow = lax.broadcasted_iota(jnp.int32, (2 * length, 512), 0) % length
    qcol = lax.broadcasted_iota(jnp.int32, (2 * length, 512), 1) % length
    diag = krow <= qcol

    def spread(tile, h):
        tile = tile.astype(jnp.float32)
        swapped = pltpu.roll(tile, HEAD, 1)
        first, second = (tile, swapped) if h % 2 == 0 else (swapped, tile)
        return jnp.concatenate([jnp.where(low, first, 0.0), jnp.where(low, 0.0, second)], axis=0).astype(jnp.bfloat16)

    def halves(stat):
        return jnp.concatenate([jnp.broadcast_to(stat[0:1], (length, 512)), jnp.broadcast_to(stat[1:2], (length, 512))], axis=0)

    def by_half(x, op):
        return jnp.concatenate([op(x[:length], axis=0, keepdims=True), op(x[length:], axis=0, keepdims=True)], axis=0)

    for h in range(4):
        t = h // 2
        for i in range(4):
            cols = slice(h * 512 + i * 128, h * 512 + (i + 1) * 128)
            q4[i * length : (i + 1) * length, :] = q_ref[:, cols]
            g4[i * length : (i + 1) * length, :] = g_ref[:, cols]

        def score_step(j, top, masked):
            keys = spread(kv_ref[j, :, t * 128 : (t + 1) * 128], h)
            kz_ref[j] = keys
            vz_ref[j] = spread(kv_ref[j, :, 256 + t * 128 : 256 + (t + 1) * 128], h)
            s = nt(keys, q4[...])
            if masked:
                s = jnp.where(diag, s, -1e30)
            s_ref[j] = s
            return jnp.maximum(top, by_half(s, jnp.max))

        top = lax.fori_loop(0, c, lambda j, m: score_step(j, m, False), jnp.full((2, 512), -1e30, jnp.float32))
        top = score_step(c, top, True)
        top_wide = halves(top)

        def sum_step(j, state):
            total, dot = state
            p = jnp.exp2((s_ref[j] - top_wide) * EXP_SCALE)
            dp = nt(vz_ref[j], g4[...])
            s_ref[j] = p
            p_ref[j] = dp
            return total + by_half(p, jnp.sum), dot + by_half(p * dp, jnp.sum)

        zero = jnp.zeros((2, 512), jnp.float32)
        total, dot = lax.fori_loop(0, c + 1, sum_step, (zero, zero))
        inverse = 1.0 / total
        inverse_wide = halves(inverse)
        delta_wide = halves(dot * inverse)
        dq4[...] = jnp.zeros_like(dq4)

        def grad_step(j, carry):
            p = s_ref[j] * inverse_wide
            ds = (p * (p_ref[j] - delta_wide)).astype(jnp.bfloat16)
            dv2[j] = nn(p.astype(jnp.bfloat16), g4[...])
            dk2[j] = nn(ds, q4[...])
            dq4[...] += tn(ds, kz_ref[j])
            return carry

        lax.fori_loop(0, c + 1, grad_step, 0)
        for i in range(4):
            cols = slice(h * 512 + i * 128, h * 512 + (i + 1) * 128)
            dq_ref[:, cols] = (dq4[i * length : (i + 1) * length, :] * SCALE).astype(jnp.bfloat16)

        def out_step(j, carry):
            for ref, base, scale in ((dk2, 0, SCALE), (dv2, 256, 1.0)):
                even, odd = ref[j, :length, :], ref[j, length:, :]
                if h % 2 == 0:
                    whole = even + pltpu.roll(odd, HEAD, 1)
                else:
                    whole = pltpu.roll(even, HEAD, 1) + odd
                whole = (whole * scale).astype(jnp.bfloat16)
                cols = slice(base + t * 128, base + (t + 1) * 128)
                if h % 2 == 0:
                    dkv_ref[j, :, cols] = whole
                else:
                    dkv_ref[j, :, cols] = jnp.where(low, dkv_ref[j, :, cols], whole)
            return carry

        lax.fori_loop(0, c + 1, out_step, 0)


ATTENTION_SCRATCH = [
    pltpu.VMEM((8, 256, 512), jnp.float32),
    pltpu.VMEM((8, 256, 512), jnp.float32),
    pltpu.VMEM((8, 256, 128), jnp.bfloat16),
    pltpu.VMEM((8, 256, 128), jnp.bfloat16),
    pltpu.VMEM((512, 128), jnp.bfloat16),
    pltpu.VMEM((512, 128), jnp.bfloat16),
    pltpu.VMEM((8, 256, 128), jnp.float32),
    pltpu.VMEM((8, 256, 128), jnp.float32),
    pltpu.VMEM((512, 128), jnp.float32),
]


def attention_kernel(*refs):
    attention_body(lax.axis_index("ctx"), *refs)


def attention_call(queries, out_grad, kv_all):
    vmem = pl.BlockSpec(memory_space=pltpu.VMEM)
    return pl.pallas_call(
        attention_kernel,
        out_shape=(
            jax.ShapeDtypeStruct(queries.shape, jnp.bfloat16),
            jax.ShapeDtypeStruct(kv_all.shape, jnp.bfloat16),
        ),
        in_specs=[vmem] * 3,
        out_specs=(vmem, vmem),
        scratch_shapes=ATTENTION_SCRATCH,
        compiler_params=pltpu.CompilerParams(vmem_limit_bytes=40 * MIB),
    )(queries, out_grad, kv_all)


def place():
    c, e = lax.axis_index("ctx"), lax.axis_index("exp")
    zh, x = c // 4, c % 4
    zl = (e // 2) % 4
    yc = (e // 8) * 2 + e % 2
    return c, e, zh, x, zh * 4 + zl, yc


def at(z, yc, x):
    return ((z // 4) * 4 + x, (yc // 2) * 8 + (z % 4) * 2 + yc % 2)


def greet(x, z, yc, c, e):
    barrier = pltpu.get_barrier_semaphore()

    def peer(i, carry):
        pl.semaphore_signal(barrier, inc=1, device_id=at((z + i // 8) % 8, (yc + i % 8) % 8, x), device_id_type=MESH)
        return carry

    lax.fori_loop(1, 64, peer, 0)
    return barrier


ORDER = (4, 3, 5, 2, 6, 1, 7, 0)


def send_kernel(pk, kv, w3, ra, rb, kv_all, w6, s_send, s_recv, f_send, f_recv, w_sem, k_send, k_recv, local):
    c, e, zh, x, z, yc = place()
    wx = x + 1 - 2 * (x % 2)
    rx = 3 - x
    barrier = greet(x, z, yc, c, e)
    for i in range(1, 4):
        pl.semaphore_signal(barrier, inc=1, device_id=(zh * 4 + (x + i) % 4, e), device_id_type=MESH)
    own_kv = pltpu.make_async_copy(kv, kv_all.at[c], local.at[0])
    own_kv.start()
    own_w = pltpu.make_async_copy(w3, w6.at[:, 0], local.at[1])
    own_w.start()
    own_rows = pltpu.make_async_copy(pk.at[e], ra.at[z * 8 + yc], local.at[2])
    own_rows.start()
    pl.semaphore_wait(barrier, 66)

    def kv_copy(src, block, i, to):
        return pltpu.make_async_remote_copy(src, kv_all.at[block], k_send.at[i], k_recv.at[block], device_id=to, device_id_type=MESH)

    other = (4 + x, e)

    @pl.when(zh == 0)
    def _():
        kv_copy(kv, c, 0, other).start()

    for i in range(1, 4):
        kv_copy(kv, c, i, (zh * 4 + (x + i) % 4, e)).start()

    weights = pltpu.make_async_remote_copy(w3, w6.at[:, 1], w_sem.at[0], w_sem.at[1], device_id=(zh * 4 + wx, e), device_id_type=MESH)
    weights.start()

    for dz in ORDER:
        zt = (z + dz) % 8

        def send_one(d, carry, zt=zt):
            yt = (yc + d) % 8
            to = at(zt, yt, x)
            pltpu.make_async_remote_copy(
                pk.at[to[1]], ra.at[z * 8 + yc], s_send, s_recv.at[z], device_id=to, device_id_type=MESH
            ).start()
            return carry

        lax.fori_loop(1 if dz == 0 else 0, 8, send_one, 0)

    @pl.when(zh == 1)
    def _():
        kv_copy(kv, x, 0, other).wait_recv()
        for i in range(1, 4):
            kv_copy(kv_all.at[x], x, 3 + i, (4 + (x + i) % 4, e)).start()

    def forward(zs):
        return pltpu.make_async_remote_copy(
            ra.at[pl.ds(zs * 8, 8)], rb.at[pl.ds(zs * 8, 8)], f_send.at[zs], f_recv.at[zs], device_id=(zh * 4 + rx, e), device_id_type=MESH
        )

    for dz in (0, 1, 7, 2, 6, 3, 5, 4):
        zs = (z + dz) % 8
        if dz == 0:
            own_rows.wait()
            pltpu.make_async_copy(ra.at[pl.ds(0, 7)], ra.at[pl.ds(0, 7)], s_recv.at[zs]).wait()
        else:
            pltpu.make_async_copy(ra.at[pl.ds(0, 8)], ra.at[pl.ds(0, 8)], s_recv.at[zs]).wait()
        forward(zs).start()

    own_kv.wait()
    own_w.wait()
    weights.wait()
    for i in range(1, 4):
        kv_copy(kv, c, i, (zh * 4 + (x + i) % 4, e)).wait_send()
        block = zh * 4 + (x + i) % 4
        kv_copy(kv, block, i, other).wait_recv()

    @pl.when(zh == 0)
    def _():
        kv_copy(kv, c, 0, other).wait_send()

    @pl.when(zh == 1)
    def _():
        for i in range(1, 4):
            kv_copy(kv, x, 3 + i, other).wait_send()
            kv_copy(kv, (x + i) % 4, 3 + i, other).wait_recv()

    most = ra.at[pl.ds(0, 63)]
    pltpu.make_async_copy(most, most, s_send).wait()
    for zs in range(8):
        forward(zs).wait()


def send_call(pk, kv, w3):
    hbm = pl.BlockSpec(memory_space=pl.ANY)
    rows = jax.ShapeDtypeStruct((64, 16, FOLD), jnp.bfloat16)
    return pl.pallas_call(
        send_kernel,
        out_shape=(
            rows,
            rows,
            jax.ShapeDtypeStruct((8, TOK, 512), jnp.bfloat16),
            jax.ShapeDtypeStruct((3, 2, PAD, WIDTH), jnp.bfloat16),
        ),
        in_specs=[hbm] * 3,
        out_specs=(hbm,) * 4,
        scratch_shapes=[
            pltpu.SemaphoreType.DMA,
            pltpu.SemaphoreType.DMA((8,)),
            pltpu.SemaphoreType.DMA((8,)),
            pltpu.SemaphoreType.DMA((8,)),
            pltpu.SemaphoreType.DMA((2,)),
            pltpu.SemaphoreType.DMA((7,)),
            pltpu.SemaphoreType.DMA((8,)),
            pltpu.SemaphoreType.DMA((3,)),
        ],
        compiler_params=pltpu.CompilerParams(collective_id=0, has_side_effects=True),
    )(pk, kv, w3)


def return_kernel(rows, eg, xg, dkv, back, w_in, dkv_in, own, theirs, r_send, r_recv, b_send, b_recv, w_sem, k_send, k_recv, local):
    c, e, zh, x, z, yc = place()
    wx = x + 1 - 2 * (x % 2)
    rx = 3 - x
    barrier = greet(x, z, yc, c, e)
    for i in range(1, 4):
        pl.semaphore_signal(barrier, inc=1, device_id=(zh * 4 + (x + i) % 4, e), device_id_type=MESH)
    for i in range(1, 4):
        pl.semaphore_signal(barrier, inc=1, device_id=((1 - zh) * 4 + (x + i) % 4, e), device_id_type=MESH)

    def load(zs):
        return pltpu.make_async_copy(rows.at[0, zs], own.at[zs], local.at[zs])

    for dz in range(8):
        load((z + dz) % 8).start()
    pl.semaphore_wait(barrier, 69)

    def swap(zs):
        return pltpu.make_async_remote_copy(
            rows.at[1, zs], theirs.at[zs], r_send.at[zs], r_recv.at[zs], device_id=(zh * 4 + rx, e), device_id_type=MESH
        )

    for dz in ORDER:
        swap((z + dz) % 8).start()
    wto = (zh * 4 + wx, e)
    w_copies = (
        pltpu.make_async_remote_copy(eg.at[:, 1], w_in.at[pl.ds(0, 2)], w_sem.at[0], w_sem.at[1], device_id=wto, device_id_type=MESH),
        pltpu.make_async_remote_copy(xg.at[1], w_in.at[2], w_sem.at[2], w_sem.at[3], device_id=wto, device_id_type=MESH),
    )
    for copy in w_copies:
        copy.start()

    def kv_copy(i, home, source):
        return pltpu.make_async_remote_copy(
            dkv.at[home], dkv_in.at[source], k_send.at[i], k_recv.at[source], device_id=(home, e), device_id_type=MESH
        )

    for i in range(1, 8):
        home = (c + i) % 8

        @pl.when(home < c)
        def _(i=i, home=home):
            kv_copy(i, home, c).start()

    own_kv = pltpu.make_async_copy(dkv.at[c], dkv_in.at[c], local.at[8])
    own_kv.start()

    for dz in ORDER:
        zs = (z + dz) % 8
        load(zs).wait()
        swap(zs).wait_recv()

        def add(d, carry, zs=zs):
            total = own[zs, d].astype(jnp.float32) + theirs[zs, d].astype(jnp.float32)
            own[zs, d] = total.astype(jnp.bfloat16)
            return carry

        lax.fori_loop(0, 8, add, 0)

        def send_one(d, carry, zs=zs):
            ys = (yc + d) % 8
            to = at(zs, ys, x)
            pltpu.make_async_remote_copy(
                own.at[zs, ys], back.at[zh * EXPERTS + e], b_send, b_recv, device_id=to, device_id_type=MESH
            ).start()
            return carry

        lax.fori_loop(1 if dz == 0 else 0, 8, send_one, 0)
        if dz == 0:
            own_back = pltpu.make_async_copy(own.at[z, yc], back.at[zh * EXPERTS + e], local.at[9])
            own_back.start()

    own_kv.wait()
    for copy in w_copies:
        copy.wait()
    for i in range(1, 8):
        partner = (c + i) % 8

        @pl.when(partner < c)
        def _(i=i, partner=partner):
            kv_copy(i, partner, c).wait_send()

        @pl.when(partner > c)
        def _(i=i, partner=partner):
            kv_copy(i, partner, partner).wait_recv()

    for zs in range(8):
        swap(zs).wait_send()
    own_back.wait()
    most = back.at[pl.ds(0, 63)]
    for sem in (b_send, b_recv):
        pltpu.make_async_copy(most, most, sem).wait()


def return_call(rows, eg, xg, dkv):
    hbm = pl.BlockSpec(memory_space=pl.ANY)
    return pl.pallas_call(
        return_kernel,
        out_shape=(
            jax.ShapeDtypeStruct((2 * EXPERTS, 16, BACK), jnp.bfloat16),
            jax.ShapeDtypeStruct((3, PAD, WIDTH), jnp.bfloat16),
            jax.ShapeDtypeStruct((8, TOK, 512), jnp.bfloat16),
        ),
        in_specs=[hbm] * 4,
        out_specs=(hbm,) * 3,
        scratch_shapes=[
            pltpu.VMEM((8, 8, 16, BACK), jnp.bfloat16),
            pltpu.VMEM((8, 8, 16, BACK), jnp.bfloat16),
            pltpu.SemaphoreType.DMA((8,)),
            pltpu.SemaphoreType.DMA((8,)),
            pltpu.SemaphoreType.DMA,
            pltpu.SemaphoreType.DMA,
            pltpu.SemaphoreType.DMA((4,)),
            pltpu.SemaphoreType.DMA((8,)),
            pltpu.SemaphoreType.DMA((8,)),
            pltpu.SemaphoreType.DMA((10,)),
        ],
        compiler_params=pltpu.CompilerParams(collective_id=1, has_side_effects=True, vmem_limit_bytes=16 * MIB),
    )(rows, eg, xg, dkv)


def pick_rows(routes, shares):
    matched = routes[:, :, None] == jnp.arange(EXPERTS)[None, None, :]
    hits = jnp.any(matched, axis=1)
    share = jnp.sum(jnp.where(matched, shares[:, :, None], 0.0), axis=1)
    before = jnp.asarray(np.tril(np.ones((TOK, TOK), np.float32), -1), jnp.bfloat16)
    earlier = jnp.dot(before, hits.astype(jnp.bfloat16), preferred_element_type=jnp.float32).astype(jnp.int32)
    row = jnp.arange(16)[None, None, :]
    chosen = hits[:, :, None] & (earlier[:, :, None] == row % CAP) & (row < 3 * CAP)
    slot_share = jnp.sum(jnp.where(chosen, share[:, :, None], 0.0), axis=0)
    return chosen, slot_share


def unfold_matrix():
    out = np.zeros((3 * 80, 256), np.float32)
    for p in range(16):
        for k in range(3):
            for s in range(CAP):
                out[k * 80 + p * CAP + s, p * 16 + k * CAP + s] = 1
    return out


UNFOLD = unfold_matrix()


def per_device(queries, key_rows, value_rows, out_grad, tokens, token_grad, route_ids, route_probs, entry_weight, exit_weight):
    f32, bf16 = jnp.float32, jnp.bfloat16
    x, g = tokens[0], token_grad[0]
    chosen, slot_share = pick_rows(route_ids[0], route_probs[0])
    part = jnp.arange(16) // CAP
    chosen3 = [(chosen & (part == k)[None, None, :]).reshape(TOK, 512).astype(bf16) for k in range(3)]

    chunks = (x[:, :FOLD], jnp.concatenate([x[:, FOLD:], g[:, FOLD:]], axis=1), g[:, :FOLD])
    packed = sum(tn(s, m) for s, m in zip(chosen3, chunks)).reshape(EXPERTS, 16, FOLD)
    is_grad = (part[:, None] == 2) | ((part[:, None] == 1) & (jnp.arange(FOLD)[None, :] >= WIDTH - FOLD))
    packed = jnp.where(is_grad[None], packed * slot_share[:, :, None], packed).astype(bf16)

    entry = entry_weight[0].transpose(1, 2, 0)
    w3 = jnp.concatenate([entry, exit_weight], axis=0)
    w3 = jnp.pad(w3, ((0, 0), (0, PAD - w3.shape[1]), (0, 0)))
    kv = jnp.concatenate([key_rows[0], value_rows[0]], axis=1)

    ra, rb, kv_all, w6 = send_call(packed, kv, w3)

    query_grad, dkv = attention_call(queries[0], out_grad[0], kv_all)

    unfold = jnp.asarray(UNFOLD, bf16)
    arrived = jnp.concatenate([ra.reshape(4, 256, FOLD), rb.reshape(4, 256, FOLD)], axis=0)
    slots = jnp.einsum("uv,bvc->buc", unfold, arrived, preferred_element_type=f32).astype(bf16)
    rest = WIDTH - FOLD
    xr = jnp.concatenate([slots[:, :80], slots[:, 80:160, :rest]], axis=2).reshape(640, WIDTH)
    gr = jnp.concatenate([slots[:, 160:], slots[:, 80:160, rest:]], axis=2).reshape(640, WIDTH)

    up_down = w6[:2].reshape(4 * PAD, WIDTH)
    leave = w6[2].reshape(2 * PAD, WIDTH)
    projected = nt(xr, up_down)
    gate, upward = projected[:, : 2 * PAD], projected[:, 2 * PAD :]
    sigma = jax.nn.sigmoid(gate)
    swish = gate * sigma
    activation = (swish * upward).astype(bf16)
    act_grad = nt(gr, leave)
    slope = sigma * (1.0 + gate * (1.0 - sigma))
    score_rows = jnp.concatenate([act_grad * upward * slope, act_grad * swish], axis=1).astype(bf16)
    row_part = nn(score_rows, up_down).astype(bf16)
    eg = tn(score_rows, xr).astype(bf16).reshape(2, 2, PAD, WIDTH)
    xg = tn(activation, gr).astype(bf16).reshape(2, PAD, WIDTH)

    row_part = jnp.pad(row_part, ((0, 0), (0, 3 * BACK - WIDTH))).reshape(8, 80, 3, BACK)
    fold = jnp.asarray(UNFOLD.reshape(3, 80, 256), bf16)
    folded = jnp.einsum("kuv,bukc->bvc", fold, row_part, preferred_element_type=f32).astype(bf16)
    folded = folded.reshape(2, 8, 8, 16, BACK)

    back, w_in, dkv_in = return_call(folded, eg, xg, dkv)

    back = back.reshape(2 * 512, BACK)
    input_grad = jnp.concatenate(
        [nn(jnp.concatenate([s, s], axis=1), back) for s in chosen3], axis=1
    )[:, :WIDTH].astype(bf16)

    c = lax.axis_index("ctx")
    later = jnp.arange(8)[:, None, None] >= c
    dkv_sum = jnp.sum(jnp.where(later, dkv_in.astype(f32), 0.0), axis=0).astype(bf16)

    hidden = exit_weight.shape[1]
    entry_grad = (eg[:, 0].astype(f32) + w_in[:2].astype(f32)).astype(bf16)[:, :hidden]
    exit_grad = (xg[0].astype(f32) + w_in[2].astype(f32)).astype(bf16)[:hidden]
    return (
        query_grad[None],
        dkv_sum[None, :, :256],
        dkv_sum[None, :, 256:],
        input_grad[None],
        entry_grad.transpose(2, 0, 1)[None],
        exit_grad[None],
    )


def solution(mesh):
    row = P("exp", "ctx", None)
    entry = P("exp", None, None, "ctx")
    return jax.shard_map(
        per_device,
        mesh=mesh,
        in_specs=(row,) * 8 + (entry, row),
        out_specs=(row,) * 4 + (entry, row),
        check_vma=False,
    )
```

```python
import functools

import jax
import jax.numpy as jnp
import numpy as np
from jax import lax
from jax.experimental import pallas as pl
from jax.experimental.pallas import tpu as pltpu
from jax.sharding import PartitionSpec as P

HEAD = 64
CAP = 5
TOK = 128
WIDTH = 2880
FOLD = 1920
BACK = 1024
PAD = 192
EXPERTS = 32
MESH = pl.DeviceIdType.MESH
MIB = 1024 * 1024
SCALE = 0.125
EXP_SCALE = 0.125 * 1.4426950408889634


def nt(a, b):
    return lax.dot_general(a, b, (((1,), (1,)), ((), ())), preferred_element_type=jnp.float32)


def tn(a, b):
    return lax.dot_general(a, b, (((0,), (0,)), ((), ())), preferred_element_type=jnp.float32)


def nn(a, b):
    return lax.dot_general(a, b, (((1,), (0,)), ((), ())), preferred_element_type=jnp.float32)


def attention_body(c, q_ref, g_ref, kv_ref, dq_ref, dkv_ref, s_ref, p_ref, kz_ref, vz_ref, q4, g4, dk2, dv2, dq4, heads=range(4)):
    length = q_ref.shape[0]
    lane = lax.broadcasted_iota(jnp.int32, (length, 128), 1)
    low = lane < HEAD
    krow = lax.broadcasted_iota(jnp.int32, (2 * length, 512), 0) % length
    qcol = lax.broadcasted_iota(jnp.int32, (2 * length, 512), 1) % length
    diag = krow <= qcol

    def spread(tile, h):
        tile = tile.astype(jnp.float32)
        swapped = pltpu.roll(tile, HEAD, 1)
        first, second = (tile, swapped) if h % 2 == 0 else (swapped, tile)
        return jnp.concatenate([jnp.where(low, first, 0.0), jnp.where(low, 0.0, second)], axis=0).astype(jnp.bfloat16)

    def halves(stat):
        return jnp.concatenate([jnp.broadcast_to(stat[0:1], (length, 512)), jnp.broadcast_to(stat[1:2], (length, 512))], axis=0)

    def by_half(x, op):
        return jnp.concatenate([op(x[:length], axis=0, keepdims=True), op(x[length:], axis=0, keepdims=True)], axis=0)

    for h in heads:
        t = h // 2
        for i in range(4):
            cols = slice(h * 512 + i * 128, h * 512 + (i + 1) * 128)
            q4[i * length : (i + 1) * length, :] = q_ref[:, cols]
            g4[i * length : (i + 1) * length, :] = g_ref[:, cols]

        def score_step(j, top, masked):
            keys = spread(kv_ref[j, :, t * 128 : (t + 1) * 128], h)
            kz_ref[j] = keys
            vz_ref[j] = spread(kv_ref[j, :, 256 + t * 128 : 256 + (t + 1) * 128], h)
            s = nt(keys, q4[...])
            if masked:
                s = jnp.where(diag, s, -1e30)
            s_ref[j] = s
            return jnp.maximum(top, by_half(s, jnp.max))

        top = lax.fori_loop(0, c, lambda j, m: score_step(j, m, False), jnp.full((2, 512), -1e30, jnp.float32))
        top = score_step(c, top, True)
        top_wide = halves(top)

        def sum_step(j, state):
            total, dot = state
            p = jnp.exp2((s_ref[j] - top_wide) * EXP_SCALE)
            dp = nt(vz_ref[j], g4[...])
            s_ref[j] = p
            p_ref[j] = dp
            return total + by_half(p, jnp.sum), dot + by_half(p * dp, jnp.sum)

        zero = jnp.zeros((2, 512), jnp.float32)
        total, dot = lax.fori_loop(0, c + 1, sum_step, (zero, zero))
        inverse = 1.0 / total
        inverse_wide = halves(inverse)
        delta_wide = halves(dot * inverse)
        dq4[...] = jnp.zeros_like(dq4)

        def grad_step(j, carry):
            p = s_ref[j] * inverse_wide
            ds = (p * (p_ref[j] - delta_wide)).astype(jnp.bfloat16)
            dv2[j] = nn(p.astype(jnp.bfloat16), g4[...])
            dk2[j] = nn(ds, q4[...])
            dq4[...] += tn(ds, kz_ref[j])
            return carry

        lax.fori_loop(0, c + 1, grad_step, 0)
        for i in range(4):
            cols = slice(h * 512 + i * 128, h * 512 + (i + 1) * 128)
            dq_ref[:, cols] = (dq4[i * length : (i + 1) * length, :] * SCALE).astype(jnp.bfloat16)

        def out_step(j, carry):
            for ref, base, scale in ((dk2, 0, SCALE), (dv2, 256, 1.0)):
                even, odd = ref[j, :length, :], ref[j, length:, :]
                if h % 2 == 0:
                    whole = even + pltpu.roll(odd, HEAD, 1)
                else:
                    whole = pltpu.roll(even, HEAD, 1) + odd
                whole = (whole * scale).astype(jnp.bfloat16)
                cols = slice(base + t * 128, base + (t + 1) * 128)
                if h % 2 == 0:
                    dkv_ref[j, :, cols] = whole
                else:
                    dkv_ref[j, :, cols] = jnp.where(low, dkv_ref[j, :, cols], whole)
            return carry

        lax.fori_loop(0, c + 1, out_step, 0)


ATTENTION_SCRATCH = [
    pltpu.VMEM((8, 256, 512), jnp.float32),
    pltpu.VMEM((8, 256, 512), jnp.float32),
    pltpu.VMEM((8, 256, 128), jnp.bfloat16),
    pltpu.VMEM((8, 256, 128), jnp.bfloat16),
    pltpu.VMEM((512, 128), jnp.bfloat16),
    pltpu.VMEM((512, 128), jnp.bfloat16),
    pltpu.VMEM((8, 256, 128), jnp.float32),
    pltpu.VMEM((8, 256, 128), jnp.float32),
    pltpu.VMEM((512, 128), jnp.float32),
]


def place():
    c, e = lax.axis_index("ctx"), lax.axis_index("exp")
    zh, x = c // 4, c % 4
    zl = (e // 2) % 4
    yc = (e // 8) * 2 + e % 2
    return c, e, zh, x, zh * 4 + zl, yc


def at(z, yc, x):
    return ((z // 4) * 4 + x, (yc // 2) * 8 + (z % 4) * 2 + yc % 2)


def greet(x, z, yc, c, e):
    barrier = pltpu.get_barrier_semaphore()

    def peer(i, carry):
        pl.semaphore_signal(barrier, inc=1, device_id=at((z + i // 8) % 8, (yc + i % 8) % 8, x), device_id_type=MESH)
        return carry

    lax.fori_loop(1, 64, peer, 0)
    return barrier


def pairs(x, e):
    core = e % 2
    near = x + 1 - 2 * (x % 2)
    far = 3 - x
    return near + core * (far - near), far + core * (near - far)


GROUPS = (1, 7, 2, 6, 0, 3, 5, 4)
SLOT = {dz: r for r, dz in enumerate(GROUPS)}
ROWS = 640


def send_kernel(
    pk, kv, gu, ex, q, g, unfold,
    xr, gr, gu2, ex2, dq, dkv,
    ra, rb, kv_all, xv, gv, s_send, s_recv, f_send, f_recv, w_sem, k_send, k_recv, local, o_sem, *scratch
):
    c, e, zh, x, z, yc = place()
    wx, rx = pairs(x, e)
    barrier = greet(x, z, yc, c, e)
    for i in range(1, 4):
        pl.semaphore_signal(barrier, inc=1, device_id=(zh * 4 + (x + i) % 4, e), device_id_type=MESH)
    own = (
        pltpu.make_async_copy(pk.at[e], ra.at[SLOT[0] * 8 + yc], local.at[0]),
        pltpu.make_async_copy(kv, kv_all.at[c], local.at[1]),
        pltpu.make_async_copy(gu, gu2.at[:, 0], local.at[2]),
        pltpu.make_async_copy(ex, ex2.at[0], local.at[3]),
    )
    for copy in own:
        copy.start()
    pl.semaphore_wait(barrier, 66)

    def kv_copy(src, block, i, to):
        return pltpu.make_async_remote_copy(src, kv_all.at[block], k_send.at[i], k_recv.at[block], device_id=to, device_id_type=MESH)

    other = (4 + x, e)

    @pl.when(zh == 0)
    def _():
        kv_copy(kv, c, 0, other).start()

    for i in range(1, 4):
        kv_copy(kv, c, i, (zh * 4 + (x + i) % 4, e)).start()

    wto = (zh * 4 + wx, e)
    weights = (
        pltpu.make_async_remote_copy(gu, gu2.at[:, 1], w_sem.at[0], w_sem.at[1], device_id=wto, device_id_type=MESH),
        pltpu.make_async_remote_copy(ex, ex2.at[1], w_sem.at[2], w_sem.at[3], device_id=wto, device_id_type=MESH),
    )
    for copy in weights:
        copy.start()

    for dz in GROUPS:
        slot = SLOT[(8 - dz) % 8]

        def send_one(d, carry, dz=dz, slot=slot):
            to = at((z + dz) % 8, (yc + d) % 8, x)
            pltpu.make_async_remote_copy(
                pk.at[to[1]], ra.at[slot * 8 + yc], s_send, s_recv.at[slot], device_id=to, device_id_type=MESH
            ).start()
            return carry

        lax.fori_loop(1 if dz == 0 else 0, 8, send_one, 0)

    @pl.when(zh == 1)
    def _():
        kv_copy(kv, x, 0, other).wait_recv()
        for i in range(1, 4):
            kv_copy(kv_all.at[x], x, 3 + i, (4 + (x + i) % 4, e)).start()

    def forward(r):
        block = pl.ds(r * 8, 8)
        return pltpu.make_async_remote_copy(
            ra.at[block], rb.at[block], f_send.at[r], f_recv.at[r], device_id=(zh * 4 + rx, e), device_id_type=MESH
        )

    def arrive(r):
        count = 8
        if GROUPS[r] == 0:
            own[0].wait()
            count = 7
        pltpu.make_async_copy(ra.at[pl.ds(0, count)], ra.at[pl.ds(0, count)], s_recv.at[r]).wait()
        forward(r).start()

    def out_copies(b):
        rows = pl.ds(b * 80, 80)
        return (
            pltpu.make_async_copy(xv.at[rows], xr.at[rows], o_sem.at[b, 0]),
            pltpu.make_async_copy(gv.at[rows], gr.at[rows], o_sem.at[b, 1]),
        )

    def spread_rows(ref, b, half):
        packets = ref[b * 16 : (b + 1) * 16].reshape(256, FOLD)
        slots = nn(unfold[...], packets)
        rest = WIDTH - FOLD
        b = b + 4 * half
        rows = slice(b * 80, (b + 1) * 80)
        xv[rows, :FOLD] = slots[:80].astype(jnp.bfloat16)
        gv[rows, :FOLD] = slots[160:].astype(jnp.bfloat16)
        xv[rows, FOLD:] = slots[80:160, :rest].astype(jnp.bfloat16)
        gv[rows, FOLD:] = slots[80:160, rest:].astype(jnp.bfloat16)
        for copy in out_copies(b):
            copy.start()

    own[1].wait()
    for i in range(1, 4):
        kv_copy(kv, zh * 4 + (x + i) % 4, i, other).wait_recv()

    @pl.when(zh == 1)
    def _():
        for i in range(1, 4):
            kv_copy(kv, (x + i) % 4, 3 + i, other).wait_recv()

    def attend(heads):
        attention_body(c, q, g, kv_all, dq, dkv, *scratch, heads=heads)

    arrive(0)
    arrive(1)
    attend((0, 1))
    arrive(2)
    arrive(3)
    attend((2, 3))
    spread_rows(ra, 0, 0)
    spread_rows(ra, 1, 0)
    arrive(4)
    arrive(5)
    spread_rows(ra, 2, 0)
    arrive(6)
    arrive(7)
    spread_rows(ra, 3, 0)
    for b in range(4):
        forward(2 * b).wait_recv()
        forward(2 * b + 1).wait_recv()
        spread_rows(rb, b, 1)

    for copy in own[2:]:
        copy.wait()
    for copy in weights:
        copy.wait()
    for i in range(1, 4):
        kv_copy(kv, c, i, other).wait_send()

    @pl.when(zh == 0)
    def _():
        kv_copy(kv, c, 0, other).wait_send()

    @pl.when(zh == 1)
    def _():
        for i in range(1, 4):
            kv_copy(kv, x, 3 + i, other).wait_send()

    most = ra.at[pl.ds(0, 63)]
    pltpu.make_async_copy(most, most, s_send).wait()
    for r in range(8):
        forward(r).wait_send()
    for b in range(8):
        for copy in out_copies(b):
            copy.wait()


def send_call(pk, kv, gu, ex, queries, out_grad):
    hbm = pl.BlockSpec(memory_space=pl.ANY)
    vmem = pl.BlockSpec(memory_space=pltpu.VMEM)
    bf16 = jnp.bfloat16
    rows = jax.ShapeDtypeStruct((ROWS, WIDTH), bf16)
    return pl.pallas_call(
        send_kernel,
        out_shape=(
            rows,
            rows,
            jax.ShapeDtypeStruct((2, 2, PAD, WIDTH), bf16),
            jax.ShapeDtypeStruct((2, PAD, WIDTH), bf16),
            jax.ShapeDtypeStruct(queries.shape, bf16),
            jax.ShapeDtypeStruct((8, TOK, 512), bf16),
        ),
        in_specs=[hbm] * 4 + [vmem] * 3,
        out_specs=(hbm,) * 4 + (vmem,) * 2,
        scratch_shapes=[
            pltpu.VMEM((64, 16, FOLD), bf16),
            pltpu.VMEM((64, 16, FOLD), bf16),
            pltpu.VMEM((8, TOK, 512), bf16),
            pltpu.VMEM((ROWS, WIDTH), bf16),
            pltpu.VMEM((ROWS, WIDTH), bf16),
            pltpu.SemaphoreType.DMA,
            pltpu.SemaphoreType.DMA((8,)),
            pltpu.SemaphoreType.DMA((8,)),
            pltpu.SemaphoreType.DMA((8,)),
            pltpu.SemaphoreType.DMA((4,)),
            pltpu.SemaphoreType.DMA((7,)),
            pltpu.SemaphoreType.DMA((8,)),
            pltpu.SemaphoreType.DMA((4,)),
            pltpu.SemaphoreType.DMA((8, 2)),
        ]
        + ATTENTION_SCRATCH,
        compiler_params=pltpu.CompilerParams(collective_id=0, has_side_effects=True, vmem_limit_bytes=52 * MIB),
    )(pk, kv, gu, ex, queries, out_grad, jnp.asarray(UNFOLD, bf16))


HOMEWARD = (7, 5, 6, 2, 3, 4, 0, 1)


def return_kernel(
    rows, eg, xg, dkv, fold,
    back, eg_in, xg_in, dkv_out,
    own, mine, theirs, kv_in, cross, r_send, r_recv, b_send, b_recv, w_sem, k_send, k_recv, local
):
    c, e, zh, x, z, yc = place()
    wx, rx = pairs(x, e)
    barrier = greet(x, z, yc, c, e)
    for i in range(1, 4):
        pl.semaphore_signal(barrier, inc=1, device_id=(zh * 4 + (x + i) % 4, e), device_id_type=MESH)

    def fold_rows(ref, b, half):
        block = slice((b + 4 * half) * 80, (b + 4 * half + 1) * 80)
        total = jnp.zeros((256, BACK), jnp.float32)
        for k in range(3):
            part = rows[block, k * BACK : min((k + 1) * BACK, WIDTH)]
            placed = nn(fold[k], part)
            if placed.shape[1] < BACK:
                placed = jnp.concatenate([placed, jnp.zeros((256, BACK - placed.shape[1]), jnp.float32)], axis=1)
            total = total + placed
        ref[b * 16 : (b + 1) * 16] = total.astype(jnp.bfloat16).reshape(16, 16, BACK)

    for b in range(4):
        fold_rows(own, b, 1)
    pl.semaphore_wait(barrier, 66)

    def swap(r):
        block = pl.ds(r * 8, 8)
        return pltpu.make_async_remote_copy(
            own.at[block], theirs.at[block], r_send.at[r], r_recv.at[r], device_id=(zh * 4 + rx, e), device_id_type=MESH
        )

    for r in HOMEWARD:
        swap(r).start()
    wto = (zh * 4 + wx, e)
    weights = (
        pltpu.make_async_remote_copy(eg.at[:, 1], eg_in, w_sem.at[0], w_sem.at[1], device_id=wto, device_id_type=MESH),
        pltpu.make_async_remote_copy(xg.at[1], xg_in, w_sem.at[2], w_sem.at[3], device_id=wto, device_id_type=MESH),
    )

    def kv_copy(i, home, slot, half):
        return pltpu.make_async_remote_copy(
            dkv.at[home], kv_in.at[slot], k_send.at[i + 3 * half], k_recv.at[slot],
            device_id=(zh * 4 + home % 4, e), device_id_type=MESH,
        )

    cross_copy = pltpu.make_async_remote_copy(
        cross, kv_in.at[8], k_send.at[0], k_recv.at[8], device_id=(x, e), device_id_type=MESH
    )

    @pl.when(zh == 1)
    def _():
        for i in range(1, 4):
            kv_copy(i, (x + i) % 4, 4 + x, 1).start()

    for i in range(1, 4):
        to = (x + i) % 4

        @pl.when(to < x)
        def _(i=i, to=to):
            kv_copy(i, zh * 4 + to, x, 0).start()

    for copy in weights:
        copy.start()

    for b in range(4):
        fold_rows(mine, b, 0)

    @pl.when(zh == 1)
    def _():
        total = dkv[x].astype(jnp.float32)
        for i in range(1, 4):
            source = 4 + (x + i) % 4
            kv_copy(i, 0, source, 1).wait_recv()
            total = total + kv_in[source].astype(jnp.float32)
        cross[...] = total.astype(jnp.bfloat16)
        cross_copy.start()

    own_back = pltpu.make_async_copy(mine.at[SLOT[0] * 8 + yc], back.at[zh * EXPERTS + e], local.at[0])
    for r in HOMEWARD:
        dz = GROUPS[r]
        swap(r).wait_recv()

        def add(d, carry, r=r):
            total = mine[r * 8 + d].astype(jnp.float32) + theirs[r * 8 + d].astype(jnp.float32)
            mine[r * 8 + d] = total.astype(jnp.bfloat16)
            return carry

        lax.fori_loop(0, 8, add, 0)

        def send_one(d, carry, r=r, dz=dz):
            ys = (yc + d) % 8
            pltpu.make_async_remote_copy(
                mine.at[r * 8 + ys], back.at[zh * EXPERTS + e], b_send, b_recv,
                device_id=at((z + dz) % 8, ys, x), device_id_type=MESH,
            ).start()
            return carry

        lax.fori_loop(1 if dz == 0 else 0, 8, send_one, 0)
        if dz == 0:
            own_back.start()

    total = [dkv[c].astype(jnp.float32)]
    for i in range(1, 4):
        source = (x + i) % 4

        @pl.when(source > x)
        def _(i=i, source=source):
            kv_copy(i, 0, source, 0).wait_recv()

        @pl.when(source < x)
        def _(i=i, source=source):
            kv_copy(i, 0, source, 0).wait_send()
            kv_in[source] = jnp.zeros((TOK, 512), jnp.bfloat16)

        total.append(kv_in[source].astype(jnp.float32))

    @pl.when(zh == 0)
    def _():
        cross_copy.wait_recv()

    @pl.when(zh == 1)
    def _():
        cross_copy.wait_send()
        for i in range(1, 4):
            kv_copy(i, 0, 0, 1).wait_send()
        kv_in[8] = jnp.zeros((TOK, 512), jnp.bfloat16)

    total.append(kv_in[8].astype(jnp.float32))
    dkv_out[...] = sum(total).astype(jnp.bfloat16)

    for copy in weights:
        copy.wait()
    for r in range(8):
        swap(r).wait_send()
    own_back.wait()
    most = back.at[pl.ds(0, 63)]
    for sem in (b_send, b_recv):
        pltpu.make_async_copy(most, most, sem).wait()


def return_call(rows, eg, xg, dkv):
    hbm = pl.BlockSpec(memory_space=pl.ANY)
    vmem = pl.BlockSpec(memory_space=pltpu.VMEM)
    bf16 = jnp.bfloat16
    packets = pltpu.VMEM((64, 16, BACK), bf16)
    return pl.pallas_call(
        return_kernel,
        out_shape=(
            jax.ShapeDtypeStruct((2 * EXPERTS, 16, BACK), bf16),
            jax.ShapeDtypeStruct((2, PAD, WIDTH), bf16),
            jax.ShapeDtypeStruct((PAD, WIDTH), bf16),
            jax.ShapeDtypeStruct((TOK, 512), bf16),
        ),
        in_specs=[vmem, hbm, hbm, vmem, vmem],
        out_specs=(hbm,) * 3 + (vmem,),
        scratch_shapes=[
            packets,
            packets,
            packets,
            pltpu.VMEM((9, TOK, 512), bf16),
            pltpu.VMEM((TOK, 512), bf16),
            pltpu.SemaphoreType.DMA((8,)),
            pltpu.SemaphoreType.DMA((8,)),
            pltpu.SemaphoreType.DMA,
            pltpu.SemaphoreType.DMA,
            pltpu.SemaphoreType.DMA((4,)),
            pltpu.SemaphoreType.DMA((7,)),
            pltpu.SemaphoreType.DMA((9,)),
            pltpu.SemaphoreType.DMA((1,)),
        ],
        compiler_params=pltpu.CompilerParams(collective_id=1, has_side_effects=True, vmem_limit_bytes=32 * MIB),
    )(rows, eg, xg, dkv, jnp.asarray(FOLDING, bf16))


def pick_rows(routes, shares):
    matched = routes[:, :, None] == jnp.arange(EXPERTS)[None, None, :]
    hits = jnp.any(matched, axis=1)
    share = jnp.sum(jnp.where(matched, shares[:, :, None], 0.0), axis=1)
    before = jnp.asarray(np.tril(np.ones((TOK, TOK), np.float32), -1), jnp.bfloat16)
    earlier = jnp.dot(before, hits.astype(jnp.bfloat16), preferred_element_type=jnp.float32).astype(jnp.int32)
    row = jnp.arange(16)[None, None, :]
    chosen = hits[:, :, None] & (earlier[:, :, None] == row % CAP) & (row < 3 * CAP)
    slot_share = jnp.sum(jnp.where(chosen, share[:, :, None], 0.0), axis=0)
    return chosen, slot_share


def unfold_matrix():
    out = np.zeros((3 * 80, 256), np.float32)
    for p in range(16):
        for k in range(3):
            for s in range(CAP):
                out[k * 80 + p * CAP + s, p * 16 + k * CAP + s] = 1
    return out


UNFOLD = unfold_matrix()
FOLDING = UNFOLD.reshape(3, 80, 256).transpose(0, 2, 1)


def per_device(queries, key_rows, value_rows, out_grad, tokens, token_grad, route_ids, route_probs, entry_weight, exit_weight):
    f32, bf16 = jnp.float32, jnp.bfloat16
    x, g = tokens[0], token_grad[0]
    chosen, slot_share = pick_rows(route_ids[0], route_probs[0])
    part = jnp.arange(16) // CAP
    chosen3 = [(chosen & (part == k)[None, None, :]).reshape(TOK, 512).astype(bf16) for k in range(3)]

    chunks = (x[:, :FOLD], jnp.concatenate([x[:, FOLD:], g[:, FOLD:]], axis=1), g[:, :FOLD])
    packed = sum(tn(s, m) for s, m in zip(chosen3, chunks)).reshape(EXPERTS, 16, FOLD)
    is_grad = (part[:, None] == 2) | ((part[:, None] == 1) & (jnp.arange(FOLD)[None, :] >= WIDTH - FOLD))
    packed = jnp.where(is_grad[None], packed * slot_share[:, :, None], packed).astype(bf16)

    hidden = exit_weight.shape[1]
    gu = jnp.pad(entry_weight[0].transpose(1, 2, 0), ((0, 0), (0, PAD - hidden), (0, 0)))
    ex = jnp.pad(exit_weight[0], ((0, PAD - hidden), (0, 0)))
    kv = jnp.concatenate([key_rows[0], value_rows[0]], axis=1)

    xr, gr, gu2, ex2, query_grad, dkv = send_call(packed, kv, gu, ex, queries[0], out_grad[0])

    up_down = gu2.reshape(4 * PAD, WIDTH)
    leave = ex2.reshape(2 * PAD, WIDTH)
    projected = nt(xr, up_down)
    gate, upward = projected[:, : 2 * PAD], projected[:, 2 * PAD :]
    sigma = jax.nn.sigmoid(gate)
    swish = gate * sigma
    activation = (swish * upward).astype(bf16)
    act_grad = nt(gr, leave)
    slope = sigma * (1.0 + gate * (1.0 - sigma))
    score_rows = jnp.concatenate([act_grad * upward * slope, act_grad * swish], axis=1).astype(bf16)
    row_part = nn(score_rows, up_down).astype(bf16)
    eg = tn(score_rows, xr).astype(bf16).reshape(2, 2, PAD, WIDTH)
    xg = tn(activation, gr).astype(bf16).reshape(2, PAD, WIDTH)

    back, eg_in, xg_in, dkv_sum = return_call(row_part, eg, xg, dkv)

    back = back.reshape(2 * 512, BACK)
    input_grad = jnp.concatenate(
        [nn(jnp.concatenate([s, s], axis=1), back) for s in chosen3], axis=1
    )[:, :WIDTH].astype(bf16)

    entry_grad = (eg[:, 0].astype(f32) + eg_in.astype(f32)).astype(bf16)[:, :hidden]
    exit_grad = (xg[0].astype(f32) + xg_in.astype(f32)).astype(bf16)[:hidden]
    return (
        query_grad[None],
        dkv_sum[None, :, :256],
        dkv_sum[None, :, 256:],
        input_grad[None],
        entry_grad.transpose(2, 0, 1)[None],
        exit_grad[None],
    )


def solution(mesh):
    row = P("exp", "ctx", None)
    entry = P("exp", None, None, "ctx")
    return jax.shard_map(
        per_device,
        mesh=mesh,
        in_specs=(row,) * 8 + (entry, row),
        out_specs=(row,) * 4 + (entry, row),
        check_vma=False,
    )
```

```python
import functools

import jax
import jax.numpy as jnp
import numpy as np
from jax import lax
from jax.experimental import pallas as pl
from jax.experimental.pallas import tpu as pltpu
from jax.sharding import PartitionSpec as P

HEAD = 64
CAP = 5
TOK = 128
WIDTH = 2880
FOLD = 1920
BACK = 1024
PAD = 192
EXPERTS = 32
MESH = pl.DeviceIdType.MESH
MIB = 1024 * 1024
SCALE = 0.125
EXP_SCALE = 0.125 * 1.4426950408889634


def nt(a, b):
    return lax.dot_general(a, b, (((1,), (1,)), ((), ())), preferred_element_type=jnp.float32)


def tn(a, b):
    return lax.dot_general(a, b, (((0,), (0,)), ((), ())), preferred_element_type=jnp.float32)


def nn(a, b):
    return lax.dot_general(a, b, (((1,), (0,)), ((), ())), preferred_element_type=jnp.float32)


def attention_body(c, q_ref, g_ref, kv_ref, dq_ref, dkv_ref, s_ref, p_ref, kz_ref, vz_ref, q4, g4, dk2, dv2, dq4, heads=range(4)):
    length = q_ref.shape[0]
    lane = lax.broadcasted_iota(jnp.int32, (length, 128), 1)
    low = lane < HEAD
    krow = lax.broadcasted_iota(jnp.int32, (2 * length, 512), 0) % length
    qcol = lax.broadcasted_iota(jnp.int32, (2 * length, 512), 1) % length
    diag = krow <= qcol

    def spread(tile, h):
        tile = tile.astype(jnp.float32)
        swapped = pltpu.roll(tile, HEAD, 1)
        first, second = (tile, swapped) if h % 2 == 0 else (swapped, tile)
        return jnp.concatenate([jnp.where(low, first, 0.0), jnp.where(low, 0.0, second)], axis=0).astype(jnp.bfloat16)

    def halves(stat):
        return jnp.concatenate([jnp.broadcast_to(stat[0:1], (length, 512)), jnp.broadcast_to(stat[1:2], (length, 512))], axis=0)

    def by_half(x, op):
        return jnp.concatenate([op(x[:length], axis=0, keepdims=True), op(x[length:], axis=0, keepdims=True)], axis=0)

    for h in heads:
        t = h // 2
        for i in range(4):
            cols = slice(h * 512 + i * 128, h * 512 + (i + 1) * 128)
            q4[i * length : (i + 1) * length, :] = q_ref[:, cols]
            g4[i * length : (i + 1) * length, :] = g_ref[:, cols]

        def score_step(j, top, masked):
            keys = spread(kv_ref[j, :, t * 128 : (t + 1) * 128], h)
            kz_ref[j] = keys
            vz_ref[j] = spread(kv_ref[j, :, 256 + t * 128 : 256 + (t + 1) * 128], h)
            s = nt(keys, q4[...])
            if masked:
                s = jnp.where(diag, s, -1e30)
            s_ref[j] = s
            return jnp.maximum(top, by_half(s, jnp.max))

        top = lax.fori_loop(0, c, lambda j, m: score_step(j, m, False), jnp.full((2, 512), -1e30, jnp.float32))
        top = score_step(c, top, True)
        top_wide = halves(top)

        def sum_step(j, state):
            total, dot = state
            p = jnp.exp2((s_ref[j] - top_wide) * EXP_SCALE)
            dp = nt(vz_ref[j], g4[...])
            s_ref[j] = p
            p_ref[j] = dp
            return total + by_half(p, jnp.sum), dot + by_half(p * dp, jnp.sum)

        zero = jnp.zeros((2, 512), jnp.float32)
        total, dot = lax.fori_loop(0, c + 1, sum_step, (zero, zero))
        inverse = 1.0 / total
        inverse_wide = halves(inverse)
        delta_wide = halves(dot * inverse)
        dq4[...] = jnp.zeros_like(dq4)

        def grad_step(j, carry):
            p = s_ref[j] * inverse_wide
            ds = (p * (p_ref[j] - delta_wide)).astype(jnp.bfloat16)
            dv2[j] = nn(p.astype(jnp.bfloat16), g4[...])
            dk2[j] = nn(ds, q4[...])
            dq4[...] += tn(ds, kz_ref[j])
            return carry

        lax.fori_loop(0, c + 1, grad_step, 0)
        for i in range(4):
            cols = slice(h * 512 + i * 128, h * 512 + (i + 1) * 128)
            dq_ref[:, cols] = (dq4[i * length : (i + 1) * length, :] * SCALE).astype(jnp.bfloat16)

        def out_step(j, carry):
            for ref, base, scale in ((dk2, 0, SCALE), (dv2, 256, 1.0)):
                even, odd = ref[j, :length, :], ref[j, length:, :]
                if h % 2 == 0:
                    whole = even + pltpu.roll(odd, HEAD, 1)
                else:
                    whole = pltpu.roll(even, HEAD, 1) + odd
                whole = (whole * scale).astype(jnp.bfloat16)
                cols = slice(base + t * 128, base + (t + 1) * 128)
                if h % 2 == 0:
                    dkv_ref[j, :, cols] = whole
                else:
                    dkv_ref[j, :, cols] = jnp.where(low, dkv_ref[j, :, cols], whole)
            return carry

        lax.fori_loop(0, c + 1, out_step, 0)


ATTENTION_SCRATCH = [
    pltpu.VMEM((8, 256, 512), jnp.float32),
    pltpu.VMEM((8, 256, 512), jnp.float32),
    pltpu.VMEM((8, 256, 128), jnp.bfloat16),
    pltpu.VMEM((8, 256, 128), jnp.bfloat16),
    pltpu.VMEM((512, 128), jnp.bfloat16),
    pltpu.VMEM((512, 128), jnp.bfloat16),
    pltpu.VMEM((8, 256, 128), jnp.float32),
    pltpu.VMEM((8, 256, 128), jnp.float32),
    pltpu.VMEM((512, 128), jnp.float32),
]


def place():
    c, e = lax.axis_index("ctx"), lax.axis_index("exp")
    zh, x = c // 4, c % 4
    zl = (e // 2) % 4
    yc = (e // 8) * 2 + e % 2
    return c, e, zh, x, zh * 4 + zl, yc


def at(z, yc, x):
    return ((z // 4) * 4 + x, (yc // 2) * 8 + (z % 4) * 2 + yc % 2)


def greet(x, z, yc, c, e):
    barrier = pltpu.get_barrier_semaphore()

    def peer(i, carry):
        pl.semaphore_signal(barrier, inc=1, device_id=at((z + i // 8) % 8, (yc + i % 8) % 8, x), device_id_type=MESH)
        return carry

    lax.fori_loop(1, 64, peer, 0)
    return barrier


def pairs(x, e):
    core = e % 2
    near = x + 1 - 2 * (x % 2)
    far = 3 - x
    return near + core * (far - near), far + core * (near - far)


GROUPS = (1, 7, 2, 6, 0, 3, 5, 4)
SLOT = {dz: r for r, dz in enumerate(GROUPS)}
ROWS = 640


HOMEWARD = ((3, 2, 1, 0), (7, 6, 5, 4))
PARTS = ((0, 1024), (1024, 1024), (2048, 896))
WIDE = 2944


def layer_kernel(
    pk, kv, gu, ex, q, g, unfold, fold,
    dq, dkv_out, back, w_out,
    ra, rb, kv_all, xv, gv, gu2, ex2, dkv, kv_in, cross, score, active, score_t, mine, own, theirs, w_own, w_in,
    s_send, s_recv, f_send, f_recv, w_sem, k_send, k_recv, d_send, d_recv,
    r_send, r_recv, b_send, b_recv, g_send, g_recv, local, *scratch
):
    f32, bf16 = jnp.float32, jnp.bfloat16
    c, e, zh, x, z, yc = place()
    wx, rx = pairs(x, e)
    rto, wto = (zh * 4 + rx, e), (zh * 4 + wx, e)
    other = (4 + x, e)
    barrier = greet(x, z, yc, c, e)
    for i in range(1, 4):
        pl.semaphore_signal(barrier, inc=1, device_id=(zh * 4 + (x + i) % 4, e), device_id_type=MESH)
    own_in = (
        pltpu.make_async_copy(pk.at[e], ra.at[SLOT[0] * 8 + yc], local.at[0]),
        pltpu.make_async_copy(kv, kv_all.at[c], local.at[1]),
        pltpu.make_async_copy(gu, gu2.at[:, 0], local.at[2]),
        pltpu.make_async_copy(ex, ex2.at[0], local.at[3]),
    )
    for copy in own_in:
        copy.start()
    pl.semaphore_wait(barrier, 66)

    def remote(src, dst, send, recv, to):
        return pltpu.make_async_remote_copy(src, dst, send, recv, device_id=to, device_id_type=MESH)

    def kv_copy(src, block, i, to):
        return remote(src, kv_all.at[block], k_send.at[i], k_recv.at[block], to)

    @pl.when(zh == 0)
    def _():
        kv_copy(kv, c, 0, other).start()

    for i in range(1, 4):
        kv_copy(kv, c, i, (zh * 4 + (x + i) % 4, e)).start()

    weights = (
        remote(gu, gu2.at[:, 1], w_sem.at[0], w_sem.at[1], wto),
        remote(ex, ex2.at[1], w_sem.at[2], w_sem.at[3], wto),
    )
    for copy in weights:
        copy.start()

    for dz in GROUPS:
        slot = SLOT[(8 - dz) % 8]

        def send_one(d, carry, dz=dz, slot=slot):
            to = at((z + dz) % 8, (yc + d) % 8, x)
            remote(pk.at[to[1]], ra.at[slot * 8 + yc], s_send, s_recv.at[slot], to).start()
            return carry

        lax.fori_loop(1 if dz == 0 else 0, 8, send_one, 0)

    @pl.when(zh == 1)
    def _():
        kv_copy(kv, x, 0, other).wait_recv()
        for i in range(1, 4):
            kv_copy(kv_all.at[x], x, 3 + i, (4 + (x + i) % 4, e)).start()

    def forward(r):
        block = pl.ds(r * 8, 8)
        return remote(ra.at[block], rb.at[block], f_send.at[r], f_recv.at[r], rto)

    def arrive(r):
        count = 8
        if GROUPS[r] == 0:
            own_in[0].wait()
            count = 7
        pltpu.make_async_copy(ra.at[pl.ds(0, count)], ra.at[pl.ds(0, count)], s_recv.at[r]).wait()
        forward(r).start()

    def spread_rows(ref, b, half):
        packets = ref[b * 16 : (b + 1) * 16].reshape(256, FOLD)
        slots = nn(unfold[...], packets)
        rest = WIDTH - FOLD
        b = b + 4 * half
        rows = slice(b * 80, (b + 1) * 80)
        xv[rows, :FOLD] = slots[:80].astype(bf16)
        gv[rows, :FOLD] = slots[160:].astype(bf16)
        xv[rows, FOLD:] = slots[80:160, :rest].astype(bf16)
        gv[rows, FOLD:] = slots[80:160, rest:].astype(bf16)

    def expert_rows(ref, b, half):
        rows = slice((b + 4 * half) * 80, (b + 4 * half + 2) * 80)
        gate = nt(xv[rows], gu2[0].reshape(2 * PAD, WIDTH))
        upward = nt(xv[rows], gu2[1].reshape(2 * PAD, WIDTH))
        act_grad = nt(gv[rows], ex2[...].reshape(2 * PAD, WIDTH))
        sigma = jax.nn.sigmoid(gate)
        swish = gate * sigma
        slope = sigma * (1.0 + gate * (1.0 - sigma))
        active[rows] = (swish * upward).astype(bf16)
        score[rows, : 2 * PAD] = (act_grad * upward * slope).astype(bf16)
        score[rows, 2 * PAD :] = (act_grad * swish).astype(bf16)
        totals = [jnp.zeros((256, BACK), f32) for _ in range(2)]
        for k in range(3):
            cols = slice(k * BACK, min((k + 1) * BACK, WIDTH))
            both = gu2[:, :, :, cols].reshape(4 * PAD, cols.stop - cols.start)
            part = nn(score[rows], both).astype(bf16)
            for i in range(2):
                placed = nn(fold[k], part[80 * i : 80 * (i + 1)])
                if placed.shape[1] < BACK:
                    placed = jnp.concatenate([placed, jnp.zeros((256, BACK - placed.shape[1]), f32)], axis=1)
                totals[i] = totals[i] + placed
        for i in range(2):
            ref[(b + i) * 16 : (b + i + 1) * 16] = totals[i].astype(bf16).reshape(16, 16, BACK)

    def swap(r):
        block = pl.ds(r * 8, 8)
        return remote(own.at[block], theirs.at[block], r_send.at[r], r_recv.at[r], rto)

    home = zh * EXPERTS + e
    own_back = pltpu.make_async_copy(mine.at[SLOT[0] * 8 + yc], back.at[home], local.at[0])

    def go_home(r):
        dz = GROUPS[r]
        swap(r).wait_recv()

        def add(d, carry):
            total = mine[r * 8 + d].astype(f32) + theirs[r * 8 + d].astype(f32)
            mine[r * 8 + d] = total.astype(bf16)
            return carry

        lax.fori_loop(0, 8, add, 0)

        def send_one(d, carry):
            ys = (yc + d) % 8
            remote(mine.at[r * 8 + ys], back.at[home], b_send, b_recv, at((z + dz) % 8, ys, x)).start()
            return carry

        lax.fori_loop(1 if dz == 0 else 0, 8, send_one, 0)
        if dz == 0:
            own_back.start()

    def dkv_copy(i, block, slot, half):
        return remote(dkv.at[block], kv_in.at[slot], d_send.at[i + 3 * half], d_recv.at[slot], (zh * 4 + block % 4, e))

    cross_copy = remote(cross, kv_in.at[8], d_send.at[0], d_recv.at[8], (x, e))

    def send_dkv():
        @pl.when(zh == 1)
        def _():
            for i in range(1, 4):
                dkv_copy(i, (x + i) % 4, 4 + x, 1).start()

        for i in range(1, 4):
            to = (x + i) % 4

            @pl.when(to < x)
            def _(i=i, to=to):
                dkv_copy(i, zh * 4 + to, x, 0).start()

    def cross_dkv():
        @pl.when(zh == 1)
        def _():
            total = dkv[x].astype(f32)
            for i in range(1, 4):
                source = 4 + (x + i) % 4
                dkv_copy(i, 0, source, 1).wait_recv()
                total = total + kv_in[source].astype(f32)
            cross[...] = total.astype(bf16)
            cross_copy.start()

    own_in[1].wait()
    for i in range(1, 4):
        kv_copy(kv, zh * 4 + (x + i) % 4, i, other).wait_recv()

    @pl.when(zh == 1)
    def _():
        for i in range(1, 4):
            kv_copy(kv, (x + i) % 4, 3 + i, other).wait_recv()

    def attend(heads):
        attention_body(c, q, g, kv_all, dq, dkv, *scratch, heads=heads)

    arrive(0)
    arrive(1)
    attend((0, 1))
    arrive(2)
    arrive(3)
    attend((2, 3))
    send_dkv()

    for copy in own_in[2:]:
        copy.wait()
    for copy in weights:
        copy.wait_recv()
    spread_rows(ra, 0, 0)
    spread_rows(ra, 1, 0)
    expert_rows(mine, 0, 0)
    for r in range(4):
        forward(r).wait_recv()
    spread_rows(rb, 0, 1)
    spread_rows(rb, 1, 1)
    expert_rows(own, 0, 1)
    for r in HOMEWARD[0]:
        swap(r).start()
    cross_dkv()
    arrive(4)
    arrive(5)
    spread_rows(ra, 2, 0)
    for r in HOMEWARD[0]:
        go_home(r)

    arrive(6)
    arrive(7)
    spread_rows(ra, 3, 0)
    expert_rows(mine, 2, 0)
    for r in range(4, 8):
        forward(r).wait_recv()
    spread_rows(rb, 2, 1)
    spread_rows(rb, 3, 1)
    expert_rows(own, 2, 1)
    for r in HOMEWARD[1]:
        swap(r).start()

    def grad_copy(t, n):
        cols = pl.ds(PARTS[n][0], PARTS[n][1])
        return remote(w_own.at[t, :, cols], w_in.at[t, :, cols], g_send.at[t, n], g_recv.at[t, n], wto)

    def weight_grads(t):
        if t < 2:
            score_t[...] = score[:, t * 2 * PAD : (t + 1) * 2 * PAD].T
        else:
            score_t[...] = active[...].T
        source = gv if t == 2 else xv
        for n, (first, count) in enumerate(PARTS):
            cols = slice(first, min(first + count, WIDTH))
            made = nn(score_t[...], source[:, cols]).astype(bf16)
            w_out[t, :, cols] = made[:PAD]
            w_own[t, :, cols] = made[PAD:]
            grad_copy(t, n).start()

    weight_grads(0)
    for r in HOMEWARD[1][:2]:
        go_home(r)
    weight_grads(1)
    for r in HOMEWARD[1][2:]:
        go_home(r)
    weight_grads(2)

    total = [dkv[c].astype(f32)]
    for i in range(1, 4):
        source = (x + i) % 4

        @pl.when(source > x)
        def _(i=i, source=source):
            dkv_copy(i, 0, source, 0).wait_recv()

        @pl.when(source < x)
        def _(i=i, source=source):
            dkv_copy(i, 0, source, 0).wait_send()
            kv_in[source] = jnp.zeros((TOK, 512), bf16)

        total.append(kv_in[source].astype(f32))

    @pl.when(zh == 0)
    def _():
        kv_copy(kv, c, 0, other).wait_send()
        cross_copy.wait_recv()

    @pl.when(zh == 1)
    def _():
        cross_copy.wait_send()
        for i in range(1, 4):
            kv_copy(kv, x, 3 + i, other).wait_send()
            dkv_copy(i, 0, 0, 1).wait_send()
        kv_in[8] = jnp.zeros((TOK, 512), bf16)

    total.append(kv_in[8].astype(f32))
    dkv_out[...] = sum(total).astype(bf16)

    for copy in weights:
        copy.wait_send()
    for i in range(1, 4):
        kv_copy(kv, c, i, other).wait_send()
    most = ra.at[pl.ds(0, 63)]
    pltpu.make_async_copy(most, most, s_send).wait()
    for r in range(8):
        forward(r).wait_send()
        swap(r).wait_send()
    for t in range(3):
        for n, (first, count) in enumerate(PARTS):
            cols = slice(first, min(first + count, WIDTH))
            grad_copy(t, n).wait()
            w_out[t, :, cols] = (w_out[t, :, cols].astype(f32) + w_in[t, :, cols].astype(f32)).astype(bf16)
    own_back.wait()
    most = back.at[pl.ds(0, 63)]
    for sem in (b_send, b_recv):
        pltpu.make_async_copy(most, most, sem).wait()


def layer_call(pk, kv, gu, ex, queries, out_grad):
    hbm = pl.BlockSpec(memory_space=pl.ANY)
    vmem = pl.BlockSpec(memory_space=pltpu.VMEM)
    bf16 = jnp.bfloat16
    dma = pltpu.SemaphoreType.DMA
    packets = pltpu.VMEM((64, 16, BACK), bf16)
    grads = pltpu.VMEM((3, PAD, WIDE), bf16)
    return pl.pallas_call(
        layer_kernel,
        out_shape=(
            jax.ShapeDtypeStruct(queries.shape, bf16),
            jax.ShapeDtypeStruct((TOK, 512), bf16),
            jax.ShapeDtypeStruct((2 * EXPERTS, 16, BACK), bf16),
            jax.ShapeDtypeStruct((3, PAD, WIDE), bf16),
        ),
        in_specs=[hbm] * 4 + [vmem] * 4,
        out_specs=(vmem, vmem, hbm, vmem),
        scratch_shapes=[
            pltpu.VMEM((64, 16, FOLD), bf16),
            pltpu.VMEM((64, 16, FOLD), bf16),
            pltpu.VMEM((8, TOK, 512), bf16),
            pltpu.VMEM((ROWS, WIDTH), bf16),
            pltpu.VMEM((ROWS, WIDTH), bf16),
            pltpu.VMEM((2, 2, PAD, WIDTH), bf16),
            pltpu.VMEM((2, PAD, WIDTH), bf16),
            pltpu.VMEM((8, TOK, 512), bf16),
            pltpu.VMEM((9, TOK, 512), bf16),
            pltpu.VMEM((TOK, 512), bf16),
            pltpu.VMEM((ROWS, 4 * PAD), bf16),
            pltpu.VMEM((ROWS, 2 * PAD), bf16),
            pltpu.VMEM((2 * PAD, ROWS), bf16),
            packets,
            packets,
            packets,
            grads,
            grads,
            dma,
            dma((8,)),
            dma((8,)),
            dma((8,)),
            dma((4,)),
            dma((7,)),
            dma((8,)),
            dma((7,)),
            dma((9,)),
            dma((8,)),
            dma((8,)),
            dma,
            dma,
            dma((3, 3)),
            dma((3, 3)),
            dma((4,)),
        ]
        + ATTENTION_SCRATCH,
        compiler_params=pltpu.CompilerParams(collective_id=0, has_side_effects=True, vmem_limit_bytes=61 * MIB),
    )(pk, kv, gu, ex, queries, out_grad, jnp.asarray(UNFOLD, bf16), jnp.asarray(FOLDING, bf16))


def pick_rows(routes, shares):
    matched = routes[:, :, None] == jnp.arange(EXPERTS)[None, None, :]
    hits = jnp.any(matched, axis=1)
    share = jnp.sum(jnp.where(matched, shares[:, :, None], 0.0), axis=1)
    before = jnp.asarray(np.tril(np.ones((TOK, TOK), np.float32), -1), jnp.bfloat16)
    earlier = jnp.dot(before, hits.astype(jnp.bfloat16), preferred_element_type=jnp.float32).astype(jnp.int32)
    row = jnp.arange(16)[None, None, :]
    chosen = hits[:, :, None] & (earlier[:, :, None] == row % CAP) & (row < 3 * CAP)
    slot_share = jnp.sum(jnp.where(chosen, share[:, :, None], 0.0), axis=0)
    return chosen, slot_share


def unfold_matrix():
    out = np.zeros((3 * 80, 256), np.float32)
    for p in range(16):
        for k in range(3):
            for s in range(CAP):
                out[k * 80 + p * CAP + s, p * 16 + k * CAP + s] = 1
    return out


UNFOLD = unfold_matrix()
FOLDING = UNFOLD.reshape(3, 80, 256).transpose(0, 2, 1)


def per_device(queries, key_rows, value_rows, out_grad, tokens, token_grad, route_ids, route_probs, entry_weight, exit_weight):
    f32, bf16 = jnp.float32, jnp.bfloat16
    x, g = tokens[0], token_grad[0]
    chosen, slot_share = pick_rows(route_ids[0], route_probs[0])
    part = jnp.arange(16) // CAP
    chosen3 = [(chosen & (part == k)[None, None, :]).reshape(TOK, 512).astype(bf16) for k in range(3)]

    chunks = (x[:, :FOLD], jnp.concatenate([x[:, FOLD:], g[:, FOLD:]], axis=1), g[:, :FOLD])
    packed = sum(tn(s, m) for s, m in zip(chosen3, chunks)).reshape(EXPERTS, 16, FOLD)
    is_grad = (part[:, None] == 2) | ((part[:, None] == 1) & (jnp.arange(FOLD)[None, :] >= WIDTH - FOLD))
    packed = jnp.where(is_grad[None], packed * slot_share[:, :, None], packed).astype(bf16)

    hidden = exit_weight.shape[1]
    gu = jnp.pad(entry_weight[0].transpose(1, 2, 0), ((0, 0), (0, PAD - hidden), (0, 0)))
    ex = jnp.pad(exit_weight[0], ((0, PAD - hidden), (0, 0)))
    kv = jnp.concatenate([key_rows[0], value_rows[0]], axis=1)

    query_grad, dkv_sum, back, w_out = layer_call(packed, kv, gu, ex, queries[0], out_grad[0])

    back = back.reshape(2 * 512, BACK)
    input_grad = jnp.concatenate(
        [nn(jnp.concatenate([s, s], axis=1), back) for s in chosen3], axis=1
    )[:, :WIDTH].astype(bf16)

    entry_grad = w_out[:2, :hidden, :WIDTH]
    exit_grad = w_out[2, :hidden, :WIDTH]
    return (
        query_grad[None],
        dkv_sum[None, :, :256],
        dkv_sum[None, :, 256:],
        input_grad[None],
        entry_grad.transpose(2, 0, 1)[None],
        exit_grad[None],
    )


def solution(mesh):
    row = P("exp", "ctx", None)
    entry = P("exp", None, None, "ctx")
    return jax.shard_map(
        per_device,
        mesh=mesh,
        in_specs=(row,) * 8 + (entry, row),
        out_specs=(row,) * 4 + (entry, row),
        check_vma=False,
    )
```

```python
import functools

import jax
import jax.numpy as jnp
import numpy as np
from jax import lax
from jax.experimental import pallas as pl
from jax.experimental.pallas import tpu as pltpu
from jax.sharding import PartitionSpec as P

HEAD = 64
CAP = 5
TOK = 128
WIDTH = 2880
FOLD = 1920
BACK = 1024
PAD = 192
EXPERTS = 32
MESH = pl.DeviceIdType.MESH
MIB = 1024 * 1024
SCALE = 0.125
EXP_SCALE = 0.125 * 1.4426950408889634


def nt(a, b):
    return lax.dot_general(a, b, (((1,), (1,)), ((), ())), preferred_element_type=jnp.float32)


def tn(a, b):
    return lax.dot_general(a, b, (((0,), (0,)), ((), ())), preferred_element_type=jnp.float32)


def nn(a, b):
    return lax.dot_general(a, b, (((1,), (0,)), ((), ())), preferred_element_type=jnp.float32)


def attention_body(c, q_ref, g_ref, kv_ref, dq_ref, dkv_ref, s_ref, kz_ref, vz_ref, q4, g4, dq4, heads=range(4)):
    length = q_ref.shape[0]
    lane = lax.broadcasted_iota(jnp.int32, (length, 128), 1)
    low = lane < HEAD
    krow = lax.broadcasted_iota(jnp.int32, (2 * length, 512), 0) % length
    qcol = lax.broadcasted_iota(jnp.int32, (2 * length, 512), 1) % length
    diag = krow <= qcol

    def spread(tile, h):
        tile = tile.astype(jnp.float32)
        swapped = pltpu.roll(tile, HEAD, 1)
        first, second = (tile, swapped) if h % 2 == 0 else (swapped, tile)
        return jnp.concatenate([jnp.where(low, first, 0.0), jnp.where(low, 0.0, second)], axis=0).astype(jnp.bfloat16)

    def halves(stat):
        return jnp.concatenate([jnp.broadcast_to(stat[0:1], (length, 512)), jnp.broadcast_to(stat[1:2], (length, 512))], axis=0)

    def by_half(x, op):
        return jnp.concatenate([op(x[:length], axis=0, keepdims=True), op(x[length:], axis=0, keepdims=True)], axis=0)

    for h in heads:
        t = h // 2
        for i in range(4):
            cols = slice(h * 512 + i * 128, h * 512 + (i + 1) * 128)
            q4[i * length : (i + 1) * length, :] = q_ref[:, cols]
            g4[i * length : (i + 1) * length, :] = g_ref[:, cols]

        def score_step(j, top, masked):
            keys = spread(kv_ref[j, :, t * 128 : (t + 1) * 128], h)
            kz_ref[j] = keys
            vz_ref[j] = spread(kv_ref[j, :, 256 + t * 128 : 256 + (t + 1) * 128], h)
            s = nt(keys, q4[...])
            if masked:
                s = jnp.where(diag, s, -1e30)
            s_ref[j] = s
            return jnp.maximum(top, by_half(s, jnp.max))

        top = lax.fori_loop(0, c, lambda j, m: score_step(j, m, False), jnp.full((2, 512), -1e30, jnp.float32))
        top = score_step(c, top, True)
        top_wide = halves(top)

        def sum_step(j, state):
            total, dot = state
            p = jnp.exp2((s_ref[j] - top_wide) * EXP_SCALE)
            dp = nt(vz_ref[j], g4[...])
            s_ref[j] = p
            return total + by_half(p, jnp.sum), dot + by_half(p * dp, jnp.sum)

        zero = jnp.zeros((2, 512), jnp.float32)
        total, dot = lax.fori_loop(0, c + 1, sum_step, (zero, zero))
        inverse = 1.0 / total
        inverse_wide = halves(inverse)
        delta_wide = halves(dot * inverse)
        dq4[...] = jnp.zeros_like(dq4)

        def place_heads(j, made, base, scale):
            even, odd = made[:length], made[length:]
            if h % 2 == 0:
                whole = even + pltpu.roll(odd, HEAD, 1)
            else:
                whole = pltpu.roll(even, HEAD, 1) + odd
            whole = (whole * scale).astype(jnp.bfloat16)
            cols = slice(base + t * 128, base + (t + 1) * 128)
            if h % 2 == 1:
                whole = jnp.where(low, dkv_ref[j, :, cols], whole)
            dkv_ref[j, :, cols] = whole

        def grad_step(j, carry):
            p = s_ref[j] * inverse_wide
            ds = (p * (nt(vz_ref[j], g4[...]) - delta_wide)).astype(jnp.bfloat16)
            place_heads(j, nn(p.astype(jnp.bfloat16), g4[...]), 256, 1.0)
            place_heads(j, nn(ds, q4[...]), 0, SCALE)
            dq4[...] += tn(ds, kz_ref[j])
            return carry

        lax.fori_loop(0, c + 1, grad_step, 0)
        for i in range(4):
            cols = slice(h * 512 + i * 128, h * 512 + (i + 1) * 128)
            dq_ref[:, cols] = (dq4[i * length : (i + 1) * length, :] * SCALE).astype(jnp.bfloat16)


ATTENTION_SCRATCH = [
    pltpu.VMEM((8, 256, 512), jnp.float32),
    pltpu.VMEM((8, 256, 128), jnp.bfloat16),
    pltpu.VMEM((8, 256, 128), jnp.bfloat16),
    pltpu.VMEM((512, 128), jnp.bfloat16),
    pltpu.VMEM((512, 128), jnp.bfloat16),
    pltpu.VMEM((512, 128), jnp.float32),
]


def place():
    c, e = lax.axis_index("ctx"), lax.axis_index("exp")
    zh, x = c // 4, c % 4
    zl = (e // 2) % 4
    yc = (e // 8) * 2 + e % 2
    return c, e, zh, x, zh * 4 + zl, yc


def at(z, yc, x):
    return ((z // 4) * 4 + x, (yc // 2) * 8 + (z % 4) * 2 + yc % 2)


def greet(x, z, yc, c, e):
    barrier = pltpu.get_barrier_semaphore()

    def peer(i, carry):
        pl.semaphore_signal(barrier, inc=1, device_id=at((z + i // 8) % 8, (yc + i % 8) % 8, x), device_id_type=MESH)
        return carry

    lax.fori_loop(1, 64, peer, 0)
    return barrier


def pairs(x, e):
    core = e % 2
    near = x + 1 - 2 * (x % 2)
    far = 3 - x
    return near + core * (far - near), far + core * (near - far)


GROUPS = (4, 0, 3, 5, 2, 6, 1, 7)
SLOT = {dz: r for r, dz in enumerate(GROUPS)}
ROWS = 640


def pack_rows(xt, gt, ids, probs, pk, chosen, wide, middle):
    f32, bf16 = jnp.float32, jnp.bfloat16
    expert = lax.broadcasted_iota(jnp.int32, (EXPERTS, TOK), 0)
    hits = jnp.zeros((EXPERTS, TOK), f32)
    share = jnp.zeros((EXPERTS, TOK), f32)
    for j in range(ids.shape[0]):
        matched = jnp.broadcast_to(ids[j : j + 1, :], (EXPERTS, TOK)) == expert
        hits = jnp.where(matched, 1.0, hits)
        share = share + jnp.where(matched, jnp.broadcast_to(probs[j : j + 1, :], (EXPERTS, TOK)), 0.0)
    before = lax.broadcasted_iota(jnp.int32, (TOK, TOK), 0) < lax.broadcasted_iota(jnp.int32, (TOK, TOK), 1)
    earlier = nn(hits.astype(bf16), jnp.where(before, 1.0, 0.0).astype(bf16))
    slot = jnp.where(hits > 0.5, earlier, -1.0)
    for e in range(EXPERTS):
        wide[0, e * 16 : (e + 1) * 16] = jnp.broadcast_to(slot[e : e + 1], (16, TOK))
        wide[1, e * 16 : (e + 1) * 16] = jnp.broadcast_to(share[e : e + 1], (16, TOK))
    row = lax.broadcasted_iota(jnp.int32, (512, TOK), 0) % 16
    slot, share = wide[0], wide[1]
    slot_share = jnp.zeros((512, TOK), f32)
    for k in range(3):
        wanted = (row - CAP * k).astype(f32)
        taken = (slot == wanted) & (row >= CAP * k) & (row < CAP * (k + 1))
        chosen[k] = jnp.where(taken, 1.0, 0.0).astype(bf16)
        slot_share = slot_share + jnp.where(taken, share, 0.0)
    wide[0] = jnp.broadcast_to(jnp.sum(slot_share, axis=1, keepdims=True), (512, TOK))
    rest = WIDTH - FOLD
    middle[:rest] = xt[FOLD:]
    middle[rest:] = gt[FOLD:]
    is_grad = lax.broadcasted_iota(jnp.int32, (TOK, FOLD), 1) >= rest
    for b in range(4):
        rows = slice(b * 128, (b + 1) * 128)
        factor = jnp.broadcast_to(wide[0, rows, :1], (TOK, FOLD))
        total = nt(chosen[0, rows], xt[:FOLD])
        total = total + nt(chosen[1, rows], middle[...]) * jnp.where(is_grad, factor, 1.0)
        total = total + nt(chosen[2, rows], gt[:FOLD]) * factor
        pk[b * 8 : (b + 1) * 8] = total.astype(bf16).reshape(8, 16, FOLD)


PARTS = ((0, 1024), (1024, 1024), (2048, 896))
WIDE = 2944


def layer_kernel(
    gu, ex, k_in, v_in, q, g, xt, gt, ids, probs, unfold, fold,
    dq, dk_out, dv_out, in_out, gu_out, ex_out,
    pk, chosen, wide, middle, back, ra, rb, kv_all, xv, gv, gu2, ex2, dkv, kv_in, cross, score, active, score_t, mine, own, theirs, w_own, w_in,
    s_send, s_recv, f_send, f_recv, w_sem, k_send, k_recv, d_send, d_recv,
    r_send, r_recv, b_send, b_recv, g_send, g_recv, local, *scratch
):
    f32, bf16 = jnp.float32, jnp.bfloat16
    c, e, zh, x, z, yc = place()
    wx, rx = pairs(x, e)
    rto, wto = (zh * 4 + rx, e), (zh * 4 + wx, e)
    other = (4 + x, e)
    barrier = greet(x, z, yc, c, e)
    for i in range(1, 4):
        pl.semaphore_signal(barrier, inc=1, device_id=(zh * 4 + (x + i) % 4, e), device_id_type=MESH)
    own_packet = pltpu.make_async_copy(pk.at[e], ra.at[SLOT[0] * 8], local.at[0])
    own_kv = (
        pltpu.make_async_copy(k_in, kv_all.at[c, :, pl.ds(0, 256)], local.at[1]),
        pltpu.make_async_copy(v_in, kv_all.at[c, :, pl.ds(256, 256)], local.at[2]),
    )
    own_in = (
        pltpu.make_async_copy(gu, gu_out, local.at[3]),
        pltpu.make_async_copy(ex, ex_out, local.at[4]),
    )
    for copy in own_kv + own_in:
        copy.start()
    kv = kv_all.at[c]
    pack_rows(xt, gt, ids, probs, pk, chosen, wide, middle)
    own_packet.start()
    hidden = ex_out.shape[0]
    gu2[:, 0, hidden:] = jnp.zeros((2, PAD - hidden, WIDTH), bf16)
    ex2[0, hidden:] = jnp.zeros((PAD - hidden, WIDTH), bf16)
    for copy in own_kv + own_in:
        copy.wait()
    gu2[:, 0, :hidden] = gu_out[...]
    ex2[0, :hidden] = ex_out[...]
    pl.semaphore_wait(barrier, 66)

    def remote(src, dst, send, recv, to):
        return pltpu.make_async_remote_copy(src, dst, send, recv, device_id=to, device_id_type=MESH)

    def kv_copy(src, block, i, to):
        return remote(src, kv_all.at[block], k_send.at[i], k_recv.at[block], to)

    @pl.when(zh == 0)
    def _():
        kv_copy(kv, c, 0, other).start()

    for i in range(1, 4):

        @pl.when((x + i) % 4 > x)
        def _(i=i):
            kv_copy(kv, c, i, (zh * 4 + (x + i) % 4, e)).start()

    weights = (
        remote(gu2.at[:, 0], gu2.at[:, 1], w_sem.at[0], w_sem.at[1], wto),
        remote(ex2.at[0], ex2.at[1], w_sem.at[2], w_sem.at[3], wto),
    )
    weights[1].start()

    for dz in GROUPS:
        slot = SLOT[(8 - dz) % 8]

        def send_one(d, carry, dz=dz, slot=slot):
            to = at((z + dz) % 8, (yc + d) % 8, x)
            remote(pk.at[to[1]], ra.at[slot * 8 + d], s_send, s_recv.at[slot * 2 + d // 4], to).start()
            return carry

        lax.fori_loop(1 if dz == 0 else 0, 8, send_one, 0)

    @pl.when(zh == 1)
    def _():
        kv_copy(kv, x, 0, other).wait_recv()
        for i in range(1, 4):
            kv_copy(kv_all.at[x], x, 3 + i, (4 + (x + i) % 4, e)).start()

    weights[0].start()

    def forward(r, half):
        block = pl.ds(r * 8 + half * 4, 4)
        i = r * 2 + half
        return remote(ra.at[block], rb.at[block], f_send.at[i], f_recv.at[i], rto)

    def arrive(r, half):
        count = 4
        if GROUPS[r] == 0 and half == 0:
            own_packet.wait()
            count = 3
        some = ra.at[pl.ds(0, count)]
        pltpu.make_async_copy(some, some, s_recv.at[r * 2 + half]).wait()
        forward(r, half).start()

    def spread_rows(ref, b, half):
        packets = ref[b * 16 : (b + 1) * 16].reshape(256, FOLD)
        slots = nn(unfold[...], packets)
        rest = WIDTH - FOLD
        b = b + 4 * half
        rows = slice(b * 80, (b + 1) * 80)
        xv[rows, :FOLD] = slots[:80].astype(bf16)
        gv[rows, :FOLD] = slots[160:].astype(bf16)
        xv[rows, FOLD:] = slots[80:160, :rest].astype(bf16)
        gv[rows, FOLD:] = slots[80:160, rest:].astype(bf16)

    def expert_rows(ref, blocks, half):
        b, size = blocks[0], len(blocks)
        rows = slice((b + 4 * half) * 80, (b + 4 * half + size) * 80)
        gate = nt(xv[rows], gu2[0].reshape(2 * PAD, WIDTH))
        upward = nt(xv[rows], gu2[1].reshape(2 * PAD, WIDTH))
        act_grad = nt(gv[rows], ex2[...].reshape(2 * PAD, WIDTH))
        sigma = jax.nn.sigmoid(gate)
        swish = gate * sigma
        slope = sigma * (1.0 + gate * (1.0 - sigma))
        active[rows] = (swish * upward).astype(bf16)
        score[rows, : 2 * PAD] = (act_grad * upward * slope).astype(bf16)
        score[rows, 2 * PAD :] = (act_grad * swish).astype(bf16)
        totals = [jnp.zeros((256, BACK), f32) for _ in range(size)]
        for k in range(3):
            cols = slice(k * BACK, min((k + 1) * BACK, WIDTH))
            both = gu2[:, :, :, cols].reshape(4 * PAD, cols.stop - cols.start)
            part = nn(score[rows], both).astype(bf16)
            for i in range(size):
                placed = nn(fold[k], part[80 * i : 80 * (i + 1)])
                if placed.shape[1] < BACK:
                    placed = jnp.concatenate([placed, jnp.zeros((256, BACK - placed.shape[1]), f32)], axis=1)
                totals[i] = totals[i] + placed
        for i in range(size):
            ref[(b + i) * 16 : (b + i + 1) * 16] = totals[i].astype(bf16).reshape(16, 16, BACK)

    def swap(r):
        block = pl.ds(r * 8, 8)
        return remote(own.at[block], theirs.at[block], r_send.at[r], r_recv.at[r], rto)

    home = zh * EXPERTS + e
    own_back = pltpu.make_async_copy(mine.at[SLOT[0] * 8], back.at[home], local.at[0])

    def go_home(r):
        dz = GROUPS[r]
        swap(r).wait_recv()

        def add(d, carry):
            total = mine[r * 8 + d].astype(f32) + theirs[r * 8 + d].astype(f32)
            mine[r * 8 + d] = total.astype(bf16)
            return carry

        lax.fori_loop(0, 8, add, 0)

        def send_one(d, carry):
            to = at((z + dz) % 8, (yc + 8 - d) % 8, x)
            remote(mine.at[r * 8 + d], back.at[home], b_send, b_recv, to).start()
            return carry

        lax.fori_loop(1 if dz == 0 else 0, 8, send_one, 0)
        if dz == 0:
            own_back.start()

    def dkv_copy(i, block, slot, half):
        return remote(dkv.at[block], kv_in.at[slot], d_send.at[i + 3 * half], d_recv.at[slot], (zh * 4 + block % 4, e))

    cross_copy = remote(cross, kv_in.at[8], d_send.at[0], d_recv.at[8], (x, e))

    def send_dkv():
        @pl.when(zh == 1)
        def _():
            for i in range(1, 4):
                dkv_copy(i, (x + i) % 4, 4 + x, 1).start()

        for i in range(1, 4):
            to = (x + i) % 4

            @pl.when(to < x)
            def _(i=i, to=to):
                dkv_copy(i, zh * 4 + to, x, 0).start()

    def cross_dkv():
        @pl.when(zh == 1)
        def _():
            total = dkv[x].astype(f32)
            for i in range(1, 4):
                source = 4 + (x + i) % 4
                dkv_copy(i, 0, source, 1).wait_recv()
                total = total + kv_in[source].astype(f32)
            cross[...] = total.astype(bf16)
            cross_copy.start()

    for i in range(1, 4):

        @pl.when((x + i) % 4 < x)
        def _(i=i):
            kv_copy(kv, zh * 4 + (x + i) % 4, i, other).wait_recv()

    @pl.when(zh == 1)
    def _():
        for i in range(1, 4):
            kv_copy(kv, (x + i) % 4, 3 + i, other).wait_recv()

    def attend(heads):
        attention_body(c, q, g, kv_all, dq, dkv, *scratch, heads=heads)

    def own_rows(b):
        spread_rows(ra, b, 0)
        expert_rows(mine, (b,), 0)

    def partner_rows(b):
        for r in (2 * b, 2 * b + 1):
            for half in range(2):
                forward(r, half).wait_recv()
        spread_rows(rb, b, 1)
        expert_rows(own, (b,), 1)
        for r in (2 * b, 2 * b + 1):
            swap(r).start()

    attend((0, 1))
    arrive(1, 0)
    arrive(1, 1)
    attend((2,))
    arrive(0, 0)
    arrive(0, 1)
    attend((3,))
    send_dkv()

    for copy in weights:
        copy.wait_recv()
    own_rows(0)
    partner_rows(0)
    for half in range(2):
        arrive(2, half)
        arrive(3, half)
    own_rows(1)
    cross_dkv()
    partner_rows(1)
    for half in range(2):
        arrive(4, half)
        arrive(5, half)
    own_rows(2)
    for r in range(4):
        go_home(r)
    for half in range(2):
        arrive(6, half)
        arrive(7, half)
    partner_rows(2)
    own_rows(3)
    for r in range(4, 6):
        go_home(r)
    partner_rows(3)

    def grad_copy(t, n):
        cols = pl.ds(PARTS[n][0], PARTS[n][1])
        return remote(w_own.at[t, :, cols], w_in.at[t, :, cols], g_send.at[t, n], g_recv.at[t, n], wto)

    def grad_out(t):
        return ex_out if t == 2 else gu_out.at[t]

    def weight_grads(t):
        if t < 2:
            score_t[...] = score[:, t * 2 * PAD : (t + 1) * 2 * PAD].T
        else:
            score_t[...] = active[...].T
        source = gv if t == 2 else xv
        for n, (first, count) in enumerate(PARTS):
            cols = slice(first, min(first + count, WIDTH))
            made = nn(score_t[...], source[:, cols]).astype(bf16)
            grad_out(t)[:, cols] = made[: gu_out.shape[1]]
            w_own[t, :, cols] = made[PAD:]
            grad_copy(t, n).start()

    weight_grads(0)
    for r in range(6, 8):
        go_home(r)
    weight_grads(1)
    weight_grads(2)

    total = [dkv[c].astype(f32)]
    for i in range(1, 4):
        source = (x + i) % 4

        @pl.when(source > x)
        def _(i=i, source=source):
            dkv_copy(i, 0, source, 0).wait_recv()

        @pl.when(source < x)
        def _(i=i, source=source):
            dkv_copy(i, 0, source, 0).wait_send()
            kv_in[source] = jnp.zeros((TOK, 512), bf16)

        total.append(kv_in[source].astype(f32))

    @pl.when(zh == 0)
    def _():
        kv_copy(kv, c, 0, other).wait_send()
        cross_copy.wait_recv()

    @pl.when(zh == 1)
    def _():
        cross_copy.wait_send()
        for i in range(1, 4):
            kv_copy(kv, x, 3 + i, other).wait_send()
            dkv_copy(i, 0, 0, 1).wait_send()
        kv_in[8] = jnp.zeros((TOK, 512), bf16)

    total.append(kv_in[8].astype(f32))
    total = sum(total).astype(bf16)
    dk_out[...] = total[:, :256]
    dv_out[...] = total[:, 256:]

    for copy in weights:
        copy.wait_send()
    for i in range(1, 4):

        @pl.when((x + i) % 4 > x)
        def _(i=i):
            kv_copy(kv, c, i, other).wait_send()

    most = ra.at[pl.ds(0, 63)]
    pltpu.make_async_copy(most, most, s_send).wait()
    for r in range(8):
        for half in range(2):
            forward(r, half).wait_send()
        swap(r).wait_send()
    own_back.wait()
    most = back.at[pl.ds(0, 63)]
    for sem in (b_recv, b_send):
        pltpu.make_async_copy(most, most, sem).wait()
    for k in range(3):
        cols = slice(k * BACK, min((k + 1) * BACK, WIDTH))
        count = cols.stop - cols.start
        both = [back[h * 32 : (h + 1) * 32, :, :count].reshape(512, count) for h in range(2)]
        in_out[cols] = (tn(chosen[k], both[0]) + tn(chosen[k], both[1])).T.astype(bf16)
    for t in range(3):
        for n, (first, count) in enumerate(PARTS):
            cols = slice(first, min(first + count, WIDTH))
            grad_copy(t, n).wait()
            made = grad_out(t)
            made[:, cols] = (made[:, cols].astype(f32) + w_in[t, : made.shape[0], cols].astype(f32)).astype(bf16)


def layer_call(gu, ex, key_rows, value_rows, queries, out_grad, xt, gt, ids, probs, hidden):
    hbm = pl.BlockSpec(memory_space=pl.ANY)
    vmem = pl.BlockSpec(memory_space=pltpu.VMEM)
    bf16 = jnp.bfloat16
    dma = pltpu.SemaphoreType.DMA
    packets = pltpu.VMEM((64, 16, BACK), bf16)
    grads = pltpu.VMEM((3, PAD, WIDE), bf16)
    return pl.pallas_call(
        layer_kernel,
        out_shape=(
            jax.ShapeDtypeStruct(queries.shape, bf16),
            jax.ShapeDtypeStruct(key_rows.shape, bf16),
            jax.ShapeDtypeStruct(key_rows.shape, bf16),
            jax.ShapeDtypeStruct(xt.shape, bf16),
            jax.ShapeDtypeStruct((2, hidden, WIDTH), bf16),
            jax.ShapeDtypeStruct((hidden, WIDTH), bf16),
        ),
        in_specs=[hbm] * 4 + [vmem] * 8,
        out_specs=(vmem,) * 6,
        scratch_shapes=[
            pltpu.VMEM((EXPERTS, 16, FOLD), bf16),
            pltpu.VMEM((3, 512, TOK), bf16),
            pltpu.VMEM((2, 512, TOK), jnp.float32),
            pltpu.VMEM((FOLD, TOK), bf16),
            packets,
            pltpu.VMEM((64, 16, FOLD), bf16),
            pltpu.VMEM((64, 16, FOLD), bf16),
            pltpu.VMEM((8, TOK, 512), bf16),
            pltpu.VMEM((ROWS, WIDTH), bf16),
            pltpu.VMEM((ROWS, WIDTH), bf16),
            pltpu.VMEM((2, 2, PAD, WIDTH), bf16),
            pltpu.VMEM((2, PAD, WIDTH), bf16),
            pltpu.VMEM((8, TOK, 512), bf16),
            pltpu.VMEM((9, TOK, 512), bf16),
            pltpu.VMEM((TOK, 512), bf16),
            pltpu.VMEM((ROWS, 4 * PAD), bf16),
            pltpu.VMEM((ROWS, 2 * PAD), bf16),
            pltpu.VMEM((2 * PAD, ROWS), bf16),
            packets,
            packets,
            packets,
            grads,
            grads,
            dma,
            dma((16,)),
            dma((16,)),
            dma((16,)),
            dma((4,)),
            dma((7,)),
            dma((8,)),
            dma((7,)),
            dma((9,)),
            dma((8,)),
            dma((8,)),
            dma,
            dma,
            dma((3, 3)),
            dma((3, 3)),
            dma((5,)),
        ]
        + ATTENTION_SCRATCH,
        compiler_params=pltpu.CompilerParams(collective_id=0, has_side_effects=True, vmem_limit_bytes=60 * MIB),
    )(
        gu, ex, key_rows, value_rows, queries, out_grad, xt, gt, ids, probs,
        jnp.asarray(UNFOLD, bf16), jnp.asarray(FOLDING, bf16),
    )


def unfold_matrix():
    out = np.zeros((3 * 80, 256), np.float32)
    for p in range(16):
        for k in range(3):
            for s in range(CAP):
                out[k * 80 + p * CAP + s, p * 16 + k * CAP + s] = 1
    return out


UNFOLD = unfold_matrix()
FOLDING = UNFOLD.reshape(3, 80, 256).transpose(0, 2, 1)


def per_device(queries, key_rows, value_rows, out_grad, tokens, token_grad, route_ids, route_probs, entry_weight, exit_weight):
    hidden = exit_weight.shape[1]
    query_grad, key_grad, value_grad, input_grad, entry_grad, exit_grad = layer_call(
        entry_weight[0].transpose(1, 2, 0), exit_weight[0], key_rows[0], value_rows[0], queries[0], out_grad[0],
        tokens[0].T, token_grad[0].T, route_ids[0].T, route_probs[0].T, hidden,
    )
    return (
        query_grad[None],
        key_grad[None],
        value_grad[None],
        input_grad.T[None],
        entry_grad.transpose(2, 0, 1)[None],
        exit_grad[None],
    )


def solution(mesh):
    row = P("exp", "ctx", None)
    entry = P("exp", None, None, "ctx")
    return jax.shard_map(
        per_device,
        mesh=mesh,
        in_specs=(row,) * 8 + (entry, row),
        out_specs=(row,) * 4 + (entry, row),
        check_vma=False,
    )
```

```python
import functools

import jax
import jax.numpy as jnp
import numpy as np
from jax import lax
from jax.experimental import pallas as pl
from jax.experimental.pallas import tpu as pltpu
from jax.sharding import PartitionSpec as P

HEAD = 64
CAP = 5
TOK = 128
WIDTH = 2880
FOLD = 1920
BACK = 1024
PAD = 192
EXPERTS = 32
MESH = pl.DeviceIdType.MESH
MIB = 1024 * 1024
SCALE = 0.125
EXP_SCALE = 0.125 * 1.4426950408889634


def nt(a, b):
    return lax.dot_general(a, b, (((1,), (1,)), ((), ())), preferred_element_type=jnp.float32)


def tn(a, b):
    return lax.dot_general(a, b, (((0,), (0,)), ((), ())), preferred_element_type=jnp.float32)


def nn(a, b):
    return lax.dot_general(a, b, (((1,), (0,)), ((), ())), preferred_element_type=jnp.float32)


def attention_body(c, q_ref, g_ref, kv_ref, dq_ref, dkv_ref, s_ref, kz_ref, vz_ref, q4, g4, dq4, heads=range(4)):
    length = q_ref.shape[0]
    lane = lax.broadcasted_iota(jnp.int32, (length, 128), 1)
    low = lane < HEAD
    krow = lax.broadcasted_iota(jnp.int32, (2 * length, 512), 0) % length
    qcol = lax.broadcasted_iota(jnp.int32, (2 * length, 512), 1) % length
    diag = krow <= qcol

    def spread(tile, h):
        tile = tile.astype(jnp.float32)
        swapped = pltpu.roll(tile, HEAD, 1)
        first, second = (tile, swapped) if h % 2 == 0 else (swapped, tile)
        return jnp.concatenate([jnp.where(low, first, 0.0), jnp.where(low, 0.0, second)], axis=0).astype(jnp.bfloat16)

    def halves(stat):
        return jnp.concatenate([jnp.broadcast_to(stat[0:1], (length, 512)), jnp.broadcast_to(stat[1:2], (length, 512))], axis=0)

    def by_half(x, op):
        return jnp.concatenate([op(x[:length], axis=0, keepdims=True), op(x[length:], axis=0, keepdims=True)], axis=0)

    for h in heads:
        t = h // 2
        for i in range(4):
            cols = slice(h * 512 + i * 128, h * 512 + (i + 1) * 128)
            q4[i * length : (i + 1) * length, :] = q_ref[:, cols]
            g4[i * length : (i + 1) * length, :] = g_ref[:, cols]

        def score_step(j, top, masked):
            keys = spread(kv_ref[j, :, t * 128 : (t + 1) * 128], h)
            kz_ref[j] = keys
            vz_ref[j] = spread(kv_ref[j, :, 256 + t * 128 : 256 + (t + 1) * 128], h)
            s = nt(keys, q4[...])
            if masked:
                s = jnp.where(diag, s, -1e30)
            s_ref[j] = s
            return jnp.maximum(top, by_half(s, jnp.max))

        top = lax.fori_loop(0, c, lambda j, m: score_step(j, m, False), jnp.full((2, 512), -1e30, jnp.float32))
        top = score_step(c, top, True)
        top_wide = halves(top)

        def sum_step(j, state):
            total, dot = state
            p = jnp.exp2((s_ref[j] - top_wide) * EXP_SCALE)
            dp = nt(vz_ref[j], g4[...])
            s_ref[j] = p
            return total + by_half(p, jnp.sum), dot + by_half(p * dp, jnp.sum)

        zero = jnp.zeros((2, 512), jnp.float32)
        total, dot = lax.fori_loop(0, c + 1, sum_step, (zero, zero))
        inverse = 1.0 / total
        inverse_wide = halves(inverse)
        delta_wide = halves(dot * inverse)
        dq4[...] = jnp.zeros_like(dq4)

        def place_heads(j, made, base, scale):
            even, odd = made[:length], made[length:]
            if h % 2 == 0:
                whole = even + pltpu.roll(odd, HEAD, 1)
            else:
                whole = pltpu.roll(even, HEAD, 1) + odd
            whole = (whole * scale).astype(jnp.bfloat16)
            cols = slice(base + t * 128, base + (t + 1) * 128)
            if h % 2 == 1:
                whole = jnp.where(low, dkv_ref[j, :, cols], whole)
            dkv_ref[j, :, cols] = whole

        def grad_step(j, carry):
            p = s_ref[j] * inverse_wide
            ds = (p * (nt(vz_ref[j], g4[...]) - delta_wide)).astype(jnp.bfloat16)
            place_heads(j, nn(p.astype(jnp.bfloat16), g4[...]), 256, 1.0)
            place_heads(j, nn(ds, q4[...]), 0, SCALE)
            dq4[...] += tn(ds, kz_ref[j])
            return carry

        lax.fori_loop(0, c + 1, grad_step, 0)
        for i in range(4):
            cols = slice(h * 512 + i * 128, h * 512 + (i + 1) * 128)
            dq_ref[:, cols] = (dq4[i * length : (i + 1) * length, :] * SCALE).astype(jnp.bfloat16)


ATTENTION_SCRATCH = [
    pltpu.VMEM((8, 256, 512), jnp.float32),
    pltpu.VMEM((8, 256, 128), jnp.bfloat16),
    pltpu.VMEM((8, 256, 128), jnp.bfloat16),
    pltpu.VMEM((512, 128), jnp.bfloat16),
    pltpu.VMEM((512, 128), jnp.bfloat16),
    pltpu.VMEM((512, 128), jnp.float32),
]


def place():
    c, e = lax.axis_index("ctx"), lax.axis_index("exp")
    zh, x = c // 4, c % 4
    zl = (e // 2) % 4
    yc = (e // 8) * 2 + e % 2
    return c, e, zh, x, zh * 4 + zl, yc


def at(z, yc, x):
    return ((z // 4) * 4 + x, (yc // 2) * 8 + (z % 4) * 2 + yc % 2)


def greet(x, z, yc, c, e):
    barrier = pltpu.get_barrier_semaphore()

    def peer(i, carry):
        pl.semaphore_signal(barrier, inc=1, device_id=at((z + i // 8) % 8, (yc + i % 8) % 8, x), device_id_type=MESH)
        return carry

    lax.fori_loop(1, 64, peer, 0)
    return barrier


def pairs(x, e):
    core = e % 2
    near = x + 1 - 2 * (x % 2)
    far = 3 - x
    return near + core * (far - near), far + core * (near - far)


GROUPS = (4, 0, 3, 5, 2, 6, 1, 7)
SLOT = {dz: r for r, dz in enumerate(GROUPS)}
ROWS = 640


def pack_rows(xt, gt, ids, probs, pk, chosen, wide, middle):
    f32, bf16 = jnp.float32, jnp.bfloat16
    expert = lax.broadcasted_iota(jnp.int32, (EXPERTS, TOK), 0)
    hits = jnp.zeros((EXPERTS, TOK), f32)
    share = jnp.zeros((EXPERTS, TOK), f32)
    for j in range(ids.shape[0]):
        matched = jnp.broadcast_to(ids[j : j + 1, :], (EXPERTS, TOK)) == expert
        hits = jnp.where(matched, 1.0, hits)
        share = share + jnp.where(matched, jnp.broadcast_to(probs[j : j + 1, :], (EXPERTS, TOK)), 0.0)
    before = lax.broadcasted_iota(jnp.int32, (TOK, TOK), 0) < lax.broadcasted_iota(jnp.int32, (TOK, TOK), 1)
    earlier = nn(hits.astype(bf16), jnp.where(before, 1.0, 0.0).astype(bf16))
    slot = jnp.where(hits > 0.5, earlier, -1.0)
    for e in range(EXPERTS):
        wide[0, e * 16 : (e + 1) * 16] = jnp.broadcast_to(slot[e : e + 1], (16, TOK))
        wide[1, e * 16 : (e + 1) * 16] = jnp.broadcast_to(share[e : e + 1], (16, TOK))
    row = lax.broadcasted_iota(jnp.int32, (512, TOK), 0) % 16
    slot, share = wide[0], wide[1]
    slot_share = jnp.zeros((512, TOK), f32)
    for k in range(3):
        wanted = (row - CAP * k).astype(f32)
        taken = (slot == wanted) & (row >= CAP * k) & (row < CAP * (k + 1))
        chosen[k] = jnp.where(taken, 1.0, 0.0).astype(bf16)
        slot_share = slot_share + jnp.where(taken, share, 0.0)
    wide[0] = jnp.broadcast_to(jnp.sum(slot_share, axis=1, keepdims=True), (512, TOK))
    rest = WIDTH - FOLD
    middle[:rest] = xt[FOLD:]
    middle[rest:] = gt[FOLD:]
    is_grad = lax.broadcasted_iota(jnp.int32, (TOK, FOLD), 1) >= rest
    for b in range(4):
        rows = slice(b * 128, (b + 1) * 128)
        factor = jnp.broadcast_to(wide[0, rows, :1], (TOK, FOLD))
        total = nt(chosen[0, rows], xt[:FOLD])
        total = total + nt(chosen[1, rows], middle[...]) * jnp.where(is_grad, factor, 1.0)
        total = total + nt(chosen[2, rows], gt[:FOLD]) * factor
        pk[b * 8 : (b + 1) * 8] = total.astype(bf16).reshape(8, 16, FOLD)


PARTS = ((0, 1024), (1024, 1024), (2048, 896))
WIDE = 2944


def layer_kernel(
    gu, ex, k_in, v_in, q, g, xt, gt, ids, probs, unfold, fold,
    dq, dk_out, dv_out, in_out, gu_out, ex_out,
    pk, chosen, wide, middle, back, ra, rb, kv_all, xv, gv, gu2, ex2, dkv, kv_in, cross, score, active, score_t, mine, own, theirs, w_own, w_in,
    s_send, s_recv, f_send, f_recv, w_sem, k_send, k_recv, d_send, d_recv,
    r_send, r_recv, b_send, b_recv, g_send, g_recv, local, *scratch
):
    f32, bf16 = jnp.float32, jnp.bfloat16
    c, e, zh, x, z, yc = place()
    wx, rx = pairs(x, e)
    rto, wto = (zh * 4 + rx, e), (zh * 4 + wx, e)
    other = (4 + x, e)
    barrier = greet(x, z, yc, c, e)
    for i in range(1, 4):
        pl.semaphore_signal(barrier, inc=1, device_id=(zh * 4 + (x + i) % 4, e), device_id_type=MESH)
    own_packet = pltpu.make_async_copy(pk.at[e], ra.at[SLOT[0] * 8], local.at[0])
    own_kv = (
        pltpu.make_async_copy(k_in, kv_all.at[c, :, pl.ds(0, 256)], local.at[1]),
        pltpu.make_async_copy(v_in, kv_all.at[c, :, pl.ds(256, 256)], local.at[2]),
    )
    own_in = (
        pltpu.make_async_copy(gu, gu_out, local.at[3]),
        pltpu.make_async_copy(ex, ex_out, local.at[4]),
    )
    for copy in own_kv + own_in:
        copy.start()
    kv = kv_all.at[c]
    pack_rows(xt, gt, ids, probs, pk, chosen, wide, middle)
    own_packet.start()
    hidden = ex_out.shape[0]
    gu2[:, 0, hidden:] = jnp.zeros((2, PAD - hidden, WIDTH), bf16)
    ex2[0, hidden:] = jnp.zeros((PAD - hidden, WIDTH), bf16)
    for copy in own_kv + own_in:
        copy.wait()
    gu2[:, 0, :hidden] = gu_out[...]
    ex2[0, :hidden] = ex_out[...]
    pl.semaphore_wait(barrier, 66)

    def remote(src, dst, send, recv, to):
        return pltpu.make_async_remote_copy(src, dst, send, recv, device_id=to, device_id_type=MESH)

    def kv_copy(src, block, i, to):
        return remote(src, kv_all.at[block], k_send.at[i], k_recv.at[block], to)

    @pl.when(zh == 0)
    def _():
        kv_copy(kv, c, 0, other).start()

    for i in range(1, 4):

        @pl.when((x + i) % 4 > x)
        def _(i=i):
            kv_copy(kv, c, i, (zh * 4 + (x + i) % 4, e)).start()

    weights = (
        remote(gu2.at[:, 0], gu2.at[:, 1], w_sem.at[0], w_sem.at[1], wto),
        remote(ex2.at[0], ex2.at[1], w_sem.at[2], w_sem.at[3], wto),
    )
    weights[1].start()

    for dz in GROUPS:
        slot = SLOT[(8 - dz) % 8]

        def send_one(d, carry, dz=dz, slot=slot):
            to = at((z + dz) % 8, (yc + d) % 8, x)
            remote(pk.at[to[1]], ra.at[slot * 8 + d], s_send, s_recv.at[slot * 2 + d // 4], to).start()
            return carry

        lax.fori_loop(1 if dz == 0 else 0, 8, send_one, 0)

    @pl.when(zh == 1)
    def _():
        kv_copy(kv, x, 0, other).wait_recv()
        for i in range(1, 4):
            kv_copy(kv_all.at[x], x, 3 + i, (4 + (x + i) % 4, e)).start()

    weights[0].start()

    def forward(r, half):
        block = pl.ds(r * 8 + half * 4, 4)
        i = r * 2 + half
        return remote(ra.at[block], rb.at[block], f_send.at[i], f_recv.at[i], rto)

    def arrive(r, half):
        count = 4
        if GROUPS[r] == 0 and half == 0:
            own_packet.wait()
            count = 3
        some = ra.at[pl.ds(0, count)]
        pltpu.make_async_copy(some, some, s_recv.at[r * 2 + half]).wait()
        forward(r, half).start()

    def spread_rows(ref, b, half):
        packets = ref[b * 16 : (b + 1) * 16].reshape(256, FOLD)
        slots = nn(unfold[...], packets)
        rest = WIDTH - FOLD
        b = b + 4 * half
        rows = slice(b * 80, (b + 1) * 80)
        xv[rows, :FOLD] = slots[:80].astype(bf16)
        gv[rows, :FOLD] = slots[160:].astype(bf16)
        xv[rows, FOLD:] = slots[80:160, :rest].astype(bf16)
        gv[rows, FOLD:] = slots[80:160, rest:].astype(bf16)

    def rows_of(part):
        b, half = part
        return slice((b + 4 * half) * 80, (b + 4 * half + 1) * 80)

    def rows_from(ref, parts):
        return jnp.concatenate([ref[rows_of(part)] for part in parts], axis=0)

    def expert_in(parts):
        rows = rows_from(xv, parts)
        gate = nt(rows, gu2[0].reshape(2 * PAD, WIDTH))
        upward = nt(rows, gu2[1].reshape(2 * PAD, WIDTH))
        act_grad = nt(rows_from(gv, parts), ex2[...].reshape(2 * PAD, WIDTH))
        sigma = jax.nn.sigmoid(gate)
        swish = gate * sigma
        slope = sigma * (1.0 + gate * (1.0 - sigma))
        made = (
            (active, slice(0, 2 * PAD), swish * upward),
            (score, slice(0, 2 * PAD), act_grad * upward * slope),
            (score, slice(2 * PAD, 4 * PAD), act_grad * swish),
        )
        for ref, cols, value in made:
            value = value.astype(bf16)
            for i, part in enumerate(parts):
                ref[rows_of(part), cols] = value[80 * i : 80 * (i + 1)]

    def expert_back(parts):
        rows = rows_from(score, parts)
        totals = [jnp.zeros((256, BACK), f32) for _ in parts]
        for k in range(3):
            cols = slice(k * BACK, min((k + 1) * BACK, WIDTH))
            both = gu2[:, :, :, cols].reshape(4 * PAD, cols.stop - cols.start)
            made = nn(rows, both).astype(bf16)
            for i in range(len(parts)):
                placed = nn(fold[k], made[80 * i : 80 * (i + 1)])
                if placed.shape[1] < BACK:
                    placed = jnp.concatenate([placed, jnp.zeros((256, BACK - placed.shape[1]), f32)], axis=1)
                totals[i] = totals[i] + placed
        for (b, half), total in zip(parts, totals):
            ref = own if half else mine
            ref[b * 16 : (b + 1) * 16] = total.astype(bf16).reshape(16, 16, BACK)

    def swap(r):
        block = pl.ds(r * 8, 8)
        return remote(own.at[block], theirs.at[block], r_send.at[r], r_recv.at[r], rto)

    home = zh * EXPERTS + e
    own_back = pltpu.make_async_copy(mine.at[SLOT[0] * 8], back.at[home], local.at[0])

    def go_home(r):
        dz = GROUPS[r]
        swap(r).wait_recv()

        def add(d, carry):
            total = mine[r * 8 + d].astype(f32) + theirs[r * 8 + d].astype(f32)
            mine[r * 8 + d] = total.astype(bf16)
            return carry

        lax.fori_loop(0, 8, add, 0)

        def send_one(d, carry):
            to = at((z + dz) % 8, (yc + 8 - d) % 8, x)
            remote(mine.at[r * 8 + d], back.at[home], b_send, b_recv, to).start()
            return carry

        lax.fori_loop(1 if dz == 0 else 0, 8, send_one, 0)
        if dz == 0:
            own_back.start()

    def dkv_copy(i, block, slot, half):
        return remote(dkv.at[block], kv_in.at[slot], d_send.at[i + 3 * half], d_recv.at[slot], (zh * 4 + block % 4, e))

    cross_copy = remote(cross, kv_in.at[8], d_send.at[0], d_recv.at[8], (x, e))

    def send_dkv():
        @pl.when(zh == 1)
        def _():
            for i in range(1, 4):
                dkv_copy(i, (x + i) % 4, 4 + x, 1).start()

        for i in range(1, 4):
            to = (x + i) % 4

            @pl.when(to < x)
            def _(i=i, to=to):
                dkv_copy(i, zh * 4 + to, x, 0).start()

    def cross_dkv():
        @pl.when(zh == 1)
        def _():
            total = dkv[x].astype(f32)
            for i in range(1, 4):
                source = 4 + (x + i) % 4
                dkv_copy(i, 0, source, 1).wait_recv()
                total = total + kv_in[source].astype(f32)
            cross[...] = total.astype(bf16)
            cross_copy.start()

    for i in range(1, 4):

        @pl.when((x + i) % 4 < x)
        def _(i=i):
            kv_copy(kv, zh * 4 + (x + i) % 4, i, other).wait_recv()

    @pl.when(zh == 1)
    def _():
        for i in range(1, 4):
            kv_copy(kv, (x + i) % 4, 3 + i, other).wait_recv()

    def attend(heads):
        attention_body(c, q, g, kv_all, dq, dkv, *scratch, heads=heads)

    def arrive_groups(b):
        for half in range(2):
            for r in (2 * b, 2 * b + 1):
                arrive(r, half)

    def take_rows(b, half):
        if half:
            for r in (2 * b, 2 * b + 1):
                for i in range(2):
                    forward(r, i).wait_recv()
        spread_rows(rb if half else ra, b, half)

    def swap_rows(b):
        for r in (2 * b, 2 * b + 1):
            swap(r).start()

    attend((0, 1))
    arrive(1, 0)
    arrive(1, 1)
    attend((2,))
    arrive(0, 0)
    arrive(0, 1)
    attend((3,))
    send_dkv()

    for copy in weights:
        copy.wait_recv()
    for b in range(2):
        if b:
            arrive_groups(b)
            cross_dkv()
        take_rows(b, 0)
        take_rows(b, 1)
        expert_in(((b, 0), (b, 1)))
        expert_back(((b, 0), (b, 1)))
        swap_rows(b)
    arrive_groups(2)
    take_rows(2, 0)
    expert_in(((2, 0),))
    expert_back(((2, 0),))
    for r in range(2):
        go_home(r)
    arrive_groups(3)
    for r in range(2, 4):
        go_home(r)
    take_rows(2, 1)
    take_rows(3, 0)
    expert_in(((2, 1), (3, 0)))
    expert_back(((2, 1), (3, 0)))
    swap_rows(2)
    take_rows(3, 1)
    expert_in(((3, 1),))

    def grad_copy(t, n):
        cols = pl.ds(PARTS[n][0], PARTS[n][1])
        return remote(w_own.at[t, :, cols], w_in.at[t, :, cols], g_send.at[t, n], g_recv.at[t, n], wto)

    def grad_out(t):
        return ex_out if t == 2 else gu_out.at[t]

    def weight_grads(t):
        if t < 2:
            score_t[...] = score[:, t * 2 * PAD : (t + 1) * 2 * PAD].T
        else:
            score_t[...] = active[...].T
        source = gv if t == 2 else xv
        for n, (first, count) in enumerate(PARTS):
            cols = slice(first, min(first + count, WIDTH))
            made = nn(score_t[...], source[:, cols]).astype(bf16)
            grad_out(t)[:, cols] = made[: gu_out.shape[1]]
            w_own[t, :, cols] = made[PAD:]
            grad_copy(t, n).start()

    weight_grads(0)
    expert_back(((3, 1),))
    swap_rows(3)
    for r in range(4, 6):
        go_home(r)
    weight_grads(1)
    weight_grads(2)
    for r in range(6, 8):
        go_home(r)

    total = [dkv[c].astype(f32)]
    for i in range(1, 4):
        source = (x + i) % 4

        @pl.when(source > x)
        def _(i=i, source=source):
            dkv_copy(i, 0, source, 0).wait_recv()

        @pl.when(source < x)
        def _(i=i, source=source):
            dkv_copy(i, 0, source, 0).wait_send()
            kv_in[source] = jnp.zeros((TOK, 512), bf16)

        total.append(kv_in[source].astype(f32))

    @pl.when(zh == 0)
    def _():
        kv_copy(kv, c, 0, other).wait_send()
        cross_copy.wait_recv()

    @pl.when(zh == 1)
    def _():
        cross_copy.wait_send()
        for i in range(1, 4):
            kv_copy(kv, x, 3 + i, other).wait_send()
            dkv_copy(i, 0, 0, 1).wait_send()
        kv_in[8] = jnp.zeros((TOK, 512), bf16)

    total.append(kv_in[8].astype(f32))
    total = sum(total).astype(bf16)
    dk_out[...] = total[:, :256]
    dv_out[...] = total[:, 256:]

    for copy in weights:
        copy.wait_send()
    for i in range(1, 4):

        @pl.when((x + i) % 4 > x)
        def _(i=i):
            kv_copy(kv, c, i, other).wait_send()

    most = ra.at[pl.ds(0, 63)]
    pltpu.make_async_copy(most, most, s_send).wait()
    for r in range(8):
        for half in range(2):
            forward(r, half).wait_send()
        swap(r).wait_send()
    def add_grads(t):
        made = grad_out(t)
        for n, (first, count) in enumerate(PARTS):
            cols = slice(first, min(first + count, WIDTH))
            grad_copy(t, n).wait()
            made[:, cols] = (made[:, cols].astype(f32) + w_in[t, : made.shape[0], cols].astype(f32)).astype(bf16)

    add_grads(0)
    own_back.wait()
    most = back.at[pl.ds(0, 63)]
    for sem in (b_recv, b_send):
        pltpu.make_async_copy(most, most, sem).wait()
    for k in range(3):
        cols = slice(k * BACK, min((k + 1) * BACK, WIDTH))
        count = cols.stop - cols.start
        both = [back[h * 32 : (h + 1) * 32, :, :count].reshape(512, count) for h in range(2)]
        in_out[cols] = (tn(chosen[k], both[0]) + tn(chosen[k], both[1])).T.astype(bf16)
    add_grads(1)
    add_grads(2)


def layer_call(gu, ex, key_rows, value_rows, queries, out_grad, xt, gt, ids, probs, hidden):
    hbm = pl.BlockSpec(memory_space=pl.ANY)
    vmem = pl.BlockSpec(memory_space=pltpu.VMEM)
    bf16 = jnp.bfloat16
    dma = pltpu.SemaphoreType.DMA
    packets = pltpu.VMEM((64, 16, BACK), bf16)
    grads = pltpu.VMEM((3, PAD, WIDE), bf16)
    return pl.pallas_call(
        layer_kernel,
        out_shape=(
            jax.ShapeDtypeStruct(queries.shape, bf16),
            jax.ShapeDtypeStruct(key_rows.shape, bf16),
            jax.ShapeDtypeStruct(key_rows.shape, bf16),
            jax.ShapeDtypeStruct(xt.shape, bf16),
            jax.ShapeDtypeStruct((2, hidden, WIDTH), bf16),
            jax.ShapeDtypeStruct((hidden, WIDTH), bf16),
        ),
        in_specs=[hbm] * 4 + [vmem] * 8,
        out_specs=(vmem,) * 6,
        scratch_shapes=[
            pltpu.VMEM((EXPERTS, 16, FOLD), bf16),
            pltpu.VMEM((3, 512, TOK), bf16),
            pltpu.VMEM((2, 512, TOK), jnp.float32),
            pltpu.VMEM((FOLD, TOK), bf16),
            packets,
            pltpu.VMEM((64, 16, FOLD), bf16),
            pltpu.VMEM((64, 16, FOLD), bf16),
            pltpu.VMEM((8, TOK, 512), bf16),
            pltpu.VMEM((ROWS, WIDTH), bf16),
            pltpu.VMEM((ROWS, WIDTH), bf16),
            pltpu.VMEM((2, 2, PAD, WIDTH), bf16),
            pltpu.VMEM((2, PAD, WIDTH), bf16),
            pltpu.VMEM((8, TOK, 512), bf16),
            pltpu.VMEM((9, TOK, 512), bf16),
            pltpu.VMEM((TOK, 512), bf16),
            pltpu.VMEM((ROWS, 4 * PAD), bf16),
            pltpu.VMEM((ROWS, 2 * PAD), bf16),
            pltpu.VMEM((2 * PAD, ROWS), bf16),
            packets,
            packets,
            packets,
            grads,
            grads,
            dma,
            dma((16,)),
            dma((16,)),
            dma((16,)),
            dma((4,)),
            dma((7,)),
            dma((8,)),
            dma((7,)),
            dma((9,)),
            dma((8,)),
            dma((8,)),
            dma,
            dma,
            dma((3, 3)),
            dma((3, 3)),
            dma((5,)),
        ]
        + ATTENTION_SCRATCH,
        compiler_params=pltpu.CompilerParams(collective_id=0, has_side_effects=True, vmem_limit_bytes=60 * MIB),
    )(
        gu, ex, key_rows, value_rows, queries, out_grad, xt, gt, ids, probs,
        jnp.asarray(UNFOLD, bf16), jnp.asarray(FOLDING, bf16),
    )


def unfold_matrix():
    out = np.zeros((3 * 80, 256), np.float32)
    for p in range(16):
        for k in range(3):
            for s in range(CAP):
                out[k * 80 + p * CAP + s, p * 16 + k * CAP + s] = 1
    return out


UNFOLD = unfold_matrix()
FOLDING = UNFOLD.reshape(3, 80, 256).transpose(0, 2, 1)


def per_device(queries, key_rows, value_rows, out_grad, tokens, token_grad, route_ids, route_probs, entry_weight, exit_weight):
    hidden = exit_weight.shape[1]
    query_grad, key_grad, value_grad, input_grad, entry_grad, exit_grad = layer_call(
        entry_weight[0].transpose(1, 2, 0), exit_weight[0], key_rows[0], value_rows[0], queries[0], out_grad[0],
        tokens[0].T, token_grad[0].T, route_ids[0].T, route_probs[0].T, hidden,
    )
    return (
        query_grad[None],
        key_grad[None],
        value_grad[None],
        input_grad.T[None],
        entry_grad.transpose(2, 0, 1)[None],
        exit_grad[None],
    )


def solution(mesh):
    row = P("exp", "ctx", None)
    entry = P("exp", None, None, "ctx")
    return jax.shard_map(
        per_device,
        mesh=mesh,
        in_specs=(row,) * 8 + (entry, row),
        out_specs=(row,) * 4 + (entry, row),
        check_vma=False,
    )
```

```python
import functools

import jax
import jax.numpy as jnp
import numpy as np
from jax import lax
from jax.experimental import pallas as pl
from jax.experimental.pallas import tpu as pltpu
from jax.sharding import PartitionSpec as P

HEAD = 64
CAP = 5
TOK = 128
WIDTH = 2880
FOLD = 1920
BACK = 1024
PAD = 192
EXPERTS = 32
MESH = pl.DeviceIdType.MESH
MIB = 1024 * 1024
SCALE = 0.125
EXP_SCALE = 0.125 * 1.4426950408889634


def nt(a, b):
    return lax.dot_general(a, b, (((1,), (1,)), ((), ())), preferred_element_type=jnp.float32)


def tn(a, b):
    return lax.dot_general(a, b, (((0,), (0,)), ((), ())), preferred_element_type=jnp.float32)


def nn(a, b):
    return lax.dot_general(a, b, (((1,), (0,)), ((), ())), preferred_element_type=jnp.float32)


def attention_body(c, q_ref, g_ref, kv_ref, dq_ref, dkv_ref, s_ref, kz_ref, vz_ref, q4, g4, dq4, heads=range(4)):
    length = q_ref.shape[0]
    lane = lax.broadcasted_iota(jnp.int32, (length, 128), 1)
    low = lane < HEAD
    krow = lax.broadcasted_iota(jnp.int32, (2 * length, 512), 0) % length
    qcol = lax.broadcasted_iota(jnp.int32, (2 * length, 512), 1) % length
    diag = krow <= qcol

    def spread(tile, h):
        tile = tile.astype(jnp.float32)
        swapped = pltpu.roll(tile, HEAD, 1)
        first, second = (tile, swapped) if h % 2 == 0 else (swapped, tile)
        return jnp.concatenate([jnp.where(low, first, 0.0), jnp.where(low, 0.0, second)], axis=0).astype(jnp.bfloat16)

    def halves(stat):
        return jnp.concatenate([jnp.broadcast_to(stat[0:1], (length, 512)), jnp.broadcast_to(stat[1:2], (length, 512))], axis=0)

    def by_half(x, op):
        return jnp.concatenate([op(x[:length], axis=0, keepdims=True), op(x[length:], axis=0, keepdims=True)], axis=0)

    for h in heads:
        t = h // 2
        for i in range(4):
            cols = slice(h * 512 + i * 128, h * 512 + (i + 1) * 128)
            q4[i * length : (i + 1) * length, :] = q_ref[:, cols]
            g4[i * length : (i + 1) * length, :] = g_ref[:, cols]

        def score_step(j, top, masked):
            keys = spread(kv_ref[j, :, t * 128 : (t + 1) * 128], h)
            kz_ref[j] = keys
            vz_ref[j] = spread(kv_ref[j, :, 256 + t * 128 : 256 + (t + 1) * 128], h)
            s = nt(keys, q4[...])
            if masked:
                s = jnp.where(diag, s, -1e30)
            s_ref[j] = s
            return jnp.maximum(top, by_half(s, jnp.max))

        top = lax.fori_loop(0, c, lambda j, m: score_step(j, m, False), jnp.full((2, 512), -1e30, jnp.float32))
        top = score_step(c, top, True)
        top_wide = halves(top)

        def sum_step(j, state):
            total, dot = state
            p = jnp.exp2((s_ref[j] - top_wide) * EXP_SCALE)
            dp = nt(vz_ref[j], g4[...])
            s_ref[j] = p
            return total + by_half(p, jnp.sum), dot + by_half(p * dp, jnp.sum)

        zero = jnp.zeros((2, 512), jnp.float32)
        total, dot = lax.fori_loop(0, c + 1, sum_step, (zero, zero))
        inverse = 1.0 / total
        inverse_wide = halves(inverse)
        delta_wide = halves(dot * inverse)
        dq4[...] = jnp.zeros_like(dq4)

        def place_heads(j, made, base, scale):
            even, odd = made[:length], made[length:]
            if h % 2 == 0:
                whole = even + pltpu.roll(odd, HEAD, 1)
            else:
                whole = pltpu.roll(even, HEAD, 1) + odd
            whole = (whole * scale).astype(jnp.bfloat16)
            cols = slice(base + t * 128, base + (t + 1) * 128)
            if h % 2 == 1:
                whole = jnp.where(low, dkv_ref[j, :, cols], whole)
            dkv_ref[j, :, cols] = whole

        def grad_step(j, carry):
            p = s_ref[j] * inverse_wide
            ds = (p * (nt(vz_ref[j], g4[...]) - delta_wide)).astype(jnp.bfloat16)
            place_heads(j, nn(p.astype(jnp.bfloat16), g4[...]), 256, 1.0)
            place_heads(j, nn(ds, q4[...]), 0, SCALE)
            dq4[...] += tn(ds, kz_ref[j])
            return carry

        lax.fori_loop(0, c + 1, grad_step, 0)
        for i in range(4):
            cols = slice(h * 512 + i * 128, h * 512 + (i + 1) * 128)
            dq_ref[:, cols] = (dq4[i * length : (i + 1) * length, :] * SCALE).astype(jnp.bfloat16)


ATTENTION_SCRATCH = [
    pltpu.VMEM((8, 256, 512), jnp.float32),
    pltpu.VMEM((8, 256, 128), jnp.bfloat16),
    pltpu.VMEM((8, 256, 128), jnp.bfloat16),
    pltpu.VMEM((512, 128), jnp.bfloat16),
    pltpu.VMEM((512, 128), jnp.bfloat16),
    pltpu.VMEM((512, 128), jnp.float32),
]


def place():
    c, e = lax.axis_index("ctx"), lax.axis_index("exp")
    zh, x = c // 4, c % 4
    zl = (e // 2) % 4
    yc = (e // 8) * 2 + e % 2
    return c, e, zh, x, zh * 4 + zl, yc


def at(z, yc, x):
    return ((z // 4) * 4 + x, (yc // 2) * 8 + (z % 4) * 2 + yc % 2)


def greet(x, z, yc, c, e):
    barrier = pltpu.get_barrier_semaphore()

    def peer(i, carry):
        pl.semaphore_signal(barrier, inc=1, device_id=at((z + i // 8) % 8, (yc + i % 8) % 8, x), device_id_type=MESH)
        return carry

    lax.fori_loop(1, 64, peer, 0)
    return barrier


def pairs(x, e):
    core = e % 2
    near = x + 1 - 2 * (x % 2)
    far = 3 - x
    return near + core * (far - near), far + core * (near - far)


GROUPS = (4, 0, 3, 5, 2, 6, 1, 7)
SLOT = {dz: r for r, dz in enumerate(GROUPS)}
ROWS = 640


def pack_rows(xt, gt, ids, probs, pk, chosen, wide, middle):
    f32, bf16 = jnp.float32, jnp.bfloat16
    expert = lax.broadcasted_iota(jnp.int32, (EXPERTS, TOK), 0)
    hits = jnp.zeros((EXPERTS, TOK), f32)
    share = jnp.zeros((EXPERTS, TOK), f32)
    for j in range(ids.shape[0]):
        matched = jnp.broadcast_to(ids[j : j + 1, :], (EXPERTS, TOK)) == expert
        hits = jnp.where(matched, 1.0, hits)
        share = share + jnp.where(matched, jnp.broadcast_to(probs[j : j + 1, :], (EXPERTS, TOK)), 0.0)
    before = lax.broadcasted_iota(jnp.int32, (TOK, TOK), 0) < lax.broadcasted_iota(jnp.int32, (TOK, TOK), 1)
    earlier = nn(hits.astype(bf16), jnp.where(before, 1.0, 0.0).astype(bf16))
    slot = jnp.where(hits > 0.5, earlier, -1.0)
    for e in range(EXPERTS):
        wide[0, e * 16 : (e + 1) * 16] = jnp.broadcast_to(slot[e : e + 1], (16, TOK))
        wide[1, e * 16 : (e + 1) * 16] = jnp.broadcast_to(share[e : e + 1], (16, TOK))
    row = lax.broadcasted_iota(jnp.int32, (512, TOK), 0) % 16
    slot, share = wide[0], wide[1]
    slot_share = jnp.zeros((512, TOK), f32)
    for k in range(3):
        wanted = (row - CAP * k).astype(f32)
        taken = (slot == wanted) & (row >= CAP * k) & (row < CAP * (k + 1))
        chosen[k] = jnp.where(taken, 1.0, 0.0).astype(bf16)
        slot_share = slot_share + jnp.where(taken, share, 0.0)
    wide[0] = jnp.broadcast_to(jnp.sum(slot_share, axis=1, keepdims=True), (512, TOK))
    rest = WIDTH - FOLD
    middle[:rest] = xt[FOLD:]
    middle[rest:] = gt[FOLD:]
    is_grad = lax.broadcasted_iota(jnp.int32, (TOK, FOLD), 1) >= rest
    for b in range(4):
        rows = slice(b * 128, (b + 1) * 128)
        factor = jnp.broadcast_to(wide[0, rows, :1], (TOK, FOLD))
        total = nt(chosen[0, rows], xt[:FOLD])
        total = total + nt(chosen[1, rows], middle[...]) * jnp.where(is_grad, factor, 1.0)
        total = total + nt(chosen[2, rows], gt[:FOLD]) * factor
        pk[b * 8 : (b + 1) * 8] = total.astype(bf16).reshape(8, 16, FOLD)


PARTS = ((0, 1024), (1024, 1024), (2048, 896))
WIDE = 2944


def layer_kernel(
    gu, ex, k_in, v_in, q, g, xt, gt, ids, probs, unfold, fold,
    dq, dk_out, dv_out, in_out, gu_out, ex_out,
    pk, chosen, wide, middle, back, ra, rb, kv_all, xv, gv, gu2, ex2, dkv, kv_in, cross, score, active, score_t, mine, own, theirs, w_own, w_in,
    s_send, s_recv, f_send, f_recv, w_sem, k_send, k_recv, d_send, d_recv,
    r_send, r_recv, b_send, b_recv, g_send, g_recv, local, *scratch
):
    f32, bf16 = jnp.float32, jnp.bfloat16
    c, e, zh, x, z, yc = place()
    wx, rx = pairs(x, e)
    rto, wto = (zh * 4 + rx, e), (zh * 4 + wx, e)
    other = (4 + x, e)
    barrier = greet(x, z, yc, c, e)
    for i in range(1, 4):
        pl.semaphore_signal(barrier, inc=1, device_id=(zh * 4 + (x + i) % 4, e), device_id_type=MESH)
    own_packet = pltpu.make_async_copy(pk.at[e], ra.at[SLOT[0] * 8], local.at[0])
    own_kv = (
        pltpu.make_async_copy(k_in, kv_all.at[c, :, pl.ds(0, 256)], local.at[1]),
        pltpu.make_async_copy(v_in, kv_all.at[c, :, pl.ds(256, 256)], local.at[2]),
    )
    own_in = (
        pltpu.make_async_copy(gu, gu_out, local.at[3]),
        pltpu.make_async_copy(ex, ex_out, local.at[4]),
    )
    for copy in own_kv + own_in:
        copy.start()
    kv = kv_all.at[c]
    pack_rows(xt, gt, ids, probs, pk, chosen, wide, middle)
    own_packet.start()
    hidden = ex_out.shape[0]
    gu2[:, 0, hidden:] = jnp.zeros((2, PAD - hidden, WIDTH), bf16)
    ex2[0, hidden:] = jnp.zeros((PAD - hidden, WIDTH), bf16)
    for copy in own_kv + own_in:
        copy.wait()
    gu2[:, 0, :hidden] = gu_out[...]
    ex2[0, :hidden] = ex_out[...]
    pl.semaphore_wait(barrier, 66)

    def remote(src, dst, send, recv, to):
        return pltpu.make_async_remote_copy(src, dst, send, recv, device_id=to, device_id_type=MESH)

    def kv_copy(src, block, i, to):
        return remote(src, kv_all.at[block], k_send.at[i], k_recv.at[block], to)

    @pl.when(zh == 0)
    def _():
        kv_copy(kv, c, 0, other).start()

    for i in range(1, 4):

        @pl.when((x + i) % 4 > x)
        def _(i=i):
            kv_copy(kv, c, i, (zh * 4 + (x + i) % 4, e)).start()

    weights = (
        remote(gu2.at[:, 0], gu2.at[:, 1], w_sem.at[0], w_sem.at[1], wto),
        remote(ex2.at[0], ex2.at[1], w_sem.at[2], w_sem.at[3], wto),
    )
    weights[1].start()

    for dz in GROUPS:
        slot = SLOT[(8 - dz) % 8]

        def send_one(d, carry, dz=dz, slot=slot):
            to = at((z + dz) % 8, (yc + d) % 8, x)
            remote(pk.at[to[1]], ra.at[slot * 8 + d], s_send, s_recv.at[slot * 2 + d // 4], to).start()
            return carry

        lax.fori_loop(1 if dz == 0 else 0, 8, send_one, 0)

    @pl.when(zh == 1)
    def _():
        kv_copy(kv, x, 0, other).wait_recv()
        for i in range(1, 4):
            kv_copy(kv_all.at[x], x, 3 + i, (4 + (x + i) % 4, e)).start()

    weights[0].start()

    def forward(r, half):
        block = pl.ds(r * 8 + half * 4, 4)
        i = r * 2 + half
        return remote(ra.at[block], rb.at[block], f_send.at[i], f_recv.at[i], rto)

    def arrive(r, half):
        count = 4
        if GROUPS[r] == 0 and half == 0:
            own_packet.wait()
            count = 3
        some = ra.at[pl.ds(0, count)]
        pltpu.make_async_copy(some, some, s_recv.at[r * 2 + half]).wait()
        forward(r, half).start()

    def spread_rows(ref, b, half):
        packets = ref[b * 16 : (b + 1) * 16].reshape(256, FOLD)
        slots = nn(unfold[...], packets)
        rest = WIDTH - FOLD
        b = b + 4 * half
        rows = slice(b * 80, (b + 1) * 80)
        xv[rows, :FOLD] = slots[:80].astype(bf16)
        gv[rows, :FOLD] = slots[160:].astype(bf16)
        xv[rows, FOLD:] = slots[80:160, :rest].astype(bf16)
        gv[rows, FOLD:] = slots[80:160, rest:].astype(bf16)

    def rows_of(part):
        b, half = part
        return slice((b + 4 * half) * 80, (b + 4 * half + 1) * 80)

    def rows_from(ref, parts):
        return jnp.concatenate([ref[rows_of(part)] for part in parts], axis=0)

    def expert_in(parts):
        rows = rows_from(xv, parts)
        gate = nt(rows, gu2[0].reshape(2 * PAD, WIDTH))
        upward = nt(rows, gu2[1].reshape(2 * PAD, WIDTH))
        act_grad = nt(rows_from(gv, parts), ex2[...].reshape(2 * PAD, WIDTH))
        sigma = jax.nn.sigmoid(gate)
        swish = gate * sigma
        slope = sigma * (1.0 + gate * (1.0 - sigma))
        made = (
            (active, slice(0, 2 * PAD), swish * upward),
            (score, slice(0, 2 * PAD), act_grad * upward * slope),
            (score, slice(2 * PAD, 4 * PAD), act_grad * swish),
        )
        for ref, cols, value in made:
            value = value.astype(bf16)
            for i, part in enumerate(parts):
                ref[rows_of(part), cols] = value[80 * i : 80 * (i + 1)]

    def expert_back(parts):
        rows = rows_from(score, parts)
        totals = [jnp.zeros((256, BACK), f32) for _ in parts]
        for k in range(3):
            cols = slice(k * BACK, min((k + 1) * BACK, WIDTH))
            both = gu2[:, :, :, cols].reshape(4 * PAD, cols.stop - cols.start)
            made = nn(rows, both).astype(bf16)
            for i in range(len(parts)):
                placed = nn(fold[k], made[80 * i : 80 * (i + 1)])
                if placed.shape[1] < BACK:
                    placed = jnp.concatenate([placed, jnp.zeros((256, BACK - placed.shape[1]), f32)], axis=1)
                totals[i] = totals[i] + placed
        for (b, half), total in zip(parts, totals):
            ref = own if half else mine
            ref[b * 16 : (b + 1) * 16] = total.astype(bf16).reshape(16, 16, BACK)

    def swap(r):
        block = pl.ds(r * 8, 8)
        return remote(own.at[block], theirs.at[block], r_send.at[r], r_recv.at[r], rto)

    home = zh * EXPERTS + e
    own_back = pltpu.make_async_copy(mine.at[SLOT[0] * 8], back.at[home], local.at[0])

    def go_home(r):
        dz = GROUPS[r]
        swap(r).wait_recv()

        def add(d, carry):
            total = mine[r * 8 + d].astype(f32) + theirs[r * 8 + d].astype(f32)
            mine[r * 8 + d] = total.astype(bf16)
            return carry

        lax.fori_loop(0, 8, add, 0)

        def send_one(d, carry):
            to = at((z + dz) % 8, (yc + 8 - d) % 8, x)
            remote(mine.at[r * 8 + d], back.at[home], b_send, b_recv, to).start()
            return carry

        lax.fori_loop(1 if dz == 0 else 0, 8, send_one, 0)
        if dz == 0:
            own_back.start()

    def dkv_copy(i, block, slot, half):
        return remote(dkv.at[block], kv_in.at[slot], d_send.at[i + 3 * half], d_recv.at[slot], (zh * 4 + block % 4, e))

    cross_copy = remote(cross, kv_in.at[8], d_send.at[0], d_recv.at[8], (x, e))

    def send_dkv():
        @pl.when(zh == 1)
        def _():
            for i in range(1, 4):
                dkv_copy(i, (x + i) % 4, 4 + x, 1).start()

        for i in range(1, 4):
            to = (x + i) % 4

            @pl.when(to < x)
            def _(i=i, to=to):
                dkv_copy(i, zh * 4 + to, x, 0).start()

    def cross_dkv():
        @pl.when(zh == 1)
        def _():
            total = dkv[x].astype(f32)
            for i in range(1, 4):
                source = 4 + (x + i) % 4
                dkv_copy(i, 0, source, 1).wait_recv()
                total = total + kv_in[source].astype(f32)
            cross[...] = total.astype(bf16)
            cross_copy.start()

    for i in range(1, 4):

        @pl.when((x + i) % 4 < x)
        def _(i=i):
            kv_copy(kv, zh * 4 + (x + i) % 4, i, other).wait_recv()

    @pl.when(zh == 1)
    def _():
        for i in range(1, 4):
            kv_copy(kv, (x + i) % 4, 3 + i, other).wait_recv()

    def attend(heads):
        attention_body(c, q, g, kv_all, dq, dkv, *scratch, heads=heads)

    def arrive_groups(b):
        for half in range(2):
            for r in (2 * b, 2 * b + 1):
                arrive(r, half)

    def take_rows(b, half):
        if half:
            for r in (2 * b, 2 * b + 1):
                for i in range(2):
                    forward(r, i).wait_recv()
        spread_rows(rb if half else ra, b, half)

    def swap_rows(b):
        for r in (2 * b, 2 * b + 1):
            swap(r).start()

    attend((0, 1))
    arrive(1, 0)
    arrive(1, 1)
    attend((2,))
    arrive(0, 0)
    arrive(0, 1)
    attend((3,))
    send_dkv()

    for copy in weights:
        copy.wait_recv()
    for b in range(2):
        if b:
            arrive_groups(b)
            cross_dkv()
        take_rows(b, 0)
        take_rows(b, 1)
        expert_in(((b, 0), (b, 1)))
        expert_back(((b, 0), (b, 1)))
        swap_rows(b)
    arrive_groups(2)
    take_rows(2, 0)
    expert_in(((2, 0),))
    expert_back(((2, 0),))
    for r in range(4):
        go_home(r)
    arrive_groups(3)
    take_rows(2, 1)
    take_rows(3, 0)
    expert_in(((2, 1), (3, 0)))
    expert_back(((2, 1), (3, 0)))
    swap_rows(2)
    take_rows(3, 1)
    expert_in(((3, 1),))

    def grad_copy(t, n):
        cols = pl.ds(PARTS[n][0], PARTS[n][1])
        return remote(w_own.at[t, :, cols], w_in.at[t, :, cols], g_send.at[t, n], g_recv.at[t, n], wto)

    def grad_out(t):
        return ex_out if t == 2 else gu_out.at[t]

    def weight_grads(t):
        if t < 2:
            score_t[...] = score[:, t * 2 * PAD : (t + 1) * 2 * PAD].T
        else:
            score_t[...] = active[...].T
        source = gv if t == 2 else xv
        for n, (first, count) in enumerate(PARTS):
            cols = slice(first, min(first + count, WIDTH))
            made = nn(score_t[...], source[:, cols]).astype(bf16)
            grad_out(t)[:, cols] = made[: gu_out.shape[1]]
            w_own[t, :, cols] = made[PAD:]
            grad_copy(t, n).start()

    weight_grads(0)
    expert_back(((3, 1),))
    swap_rows(3)
    for r in range(4, 6):
        go_home(r)
    weight_grads(1)
    weight_grads(2)
    for r in range(6, 8):
        go_home(r)

    total = [dkv[c].astype(f32)]
    for i in range(1, 4):
        source = (x + i) % 4

        @pl.when(source > x)
        def _(i=i, source=source):
            dkv_copy(i, 0, source, 0).wait_recv()

        @pl.when(source < x)
        def _(i=i, source=source):
            dkv_copy(i, 0, source, 0).wait_send()
            kv_in[source] = jnp.zeros((TOK, 512), bf16)

        total.append(kv_in[source].astype(f32))

    @pl.when(zh == 0)
    def _():
        kv_copy(kv, c, 0, other).wait_send()
        cross_copy.wait_recv()

    @pl.when(zh == 1)
    def _():
        cross_copy.wait_send()
        for i in range(1, 4):
            kv_copy(kv, x, 3 + i, other).wait_send()
            dkv_copy(i, 0, 0, 1).wait_send()
        kv_in[8] = jnp.zeros((TOK, 512), bf16)

    total.append(kv_in[8].astype(f32))
    total = sum(total).astype(bf16)
    dk_out[...] = total[:, :256]
    dv_out[...] = total[:, 256:]

    for copy in weights:
        copy.wait_send()
    for i in range(1, 4):

        @pl.when((x + i) % 4 > x)
        def _(i=i):
            kv_copy(kv, c, i, other).wait_send()

    most = ra.at[pl.ds(0, 63)]
    pltpu.make_async_copy(most, most, s_send).wait()
    for r in range(8):
        for half in range(2):
            forward(r, half).wait_send()
        swap(r).wait_send()
    own_back.wait()
    most = back.at[pl.ds(0, 63)]
    for sem in (b_recv, b_send):
        pltpu.make_async_copy(most, most, sem).wait()
    for k in range(3):
        cols = slice(k * BACK, min((k + 1) * BACK, WIDTH))
        count = cols.stop - cols.start
        both = [back[h * 32 : (h + 1) * 32, :, :count].reshape(512, count) for h in range(2)]
        in_out[cols] = (tn(chosen[k], both[0]) + tn(chosen[k], both[1])).T.astype(bf16)
    for t in range(3):
        for n, (first, count) in enumerate(PARTS):
            cols = slice(first, min(first + count, WIDTH))
            grad_copy(t, n).wait()
            made = grad_out(t)
            made[:, cols] = (made[:, cols].astype(f32) + w_in[t, : made.shape[0], cols].astype(f32)).astype(bf16)


def layer_call(gu, ex, key_rows, value_rows, queries, out_grad, xt, gt, ids, probs, hidden):
    hbm = pl.BlockSpec(memory_space=pl.ANY)
    vmem = pl.BlockSpec(memory_space=pltpu.VMEM)
    bf16 = jnp.bfloat16
    dma = pltpu.SemaphoreType.DMA
    packets = pltpu.VMEM((64, 16, BACK), bf16)
    grads = pltpu.VMEM((3, PAD, WIDE), bf16)
    return pl.pallas_call(
        layer_kernel,
        out_shape=(
            jax.ShapeDtypeStruct(queries.shape, bf16),
            jax.ShapeDtypeStruct(key_rows.shape, bf16),
            jax.ShapeDtypeStruct(key_rows.shape, bf16),
            jax.ShapeDtypeStruct(xt.shape, bf16),
            jax.ShapeDtypeStruct((2, hidden, WIDTH), bf16),
            jax.ShapeDtypeStruct((hidden, WIDTH), bf16),
        ),
        in_specs=[hbm] * 4 + [vmem] * 8,
        out_specs=(vmem,) * 6,
        scratch_shapes=[
            pltpu.VMEM((EXPERTS, 16, FOLD), bf16),
            pltpu.VMEM((3, 512, TOK), bf16),
            pltpu.VMEM((2, 512, TOK), jnp.float32),
            pltpu.VMEM((FOLD, TOK), bf16),
            packets,
            pltpu.VMEM((64, 16, FOLD), bf16),
            pltpu.VMEM((64, 16, FOLD), bf16),
            pltpu.VMEM((8, TOK, 512), bf16),
            pltpu.VMEM((ROWS, WIDTH), bf16),
            pltpu.VMEM((ROWS, WIDTH), bf16),
            pltpu.VMEM((2, 2, PAD, WIDTH), bf16),
            pltpu.VMEM((2, PAD, WIDTH), bf16),
            pltpu.VMEM((8, TOK, 512), bf16),
            pltpu.VMEM((9, TOK, 512), bf16),
            pltpu.VMEM((TOK, 512), bf16),
            pltpu.VMEM((ROWS, 4 * PAD), bf16),
            pltpu.VMEM((ROWS, 2 * PAD), bf16),
            pltpu.VMEM((2 * PAD, ROWS), bf16),
            packets,
            packets,
            packets,
            grads,
            grads,
            dma,
            dma((16,)),
            dma((16,)),
            dma((16,)),
            dma((4,)),
            dma((7,)),
            dma((8,)),
            dma((7,)),
            dma((9,)),
            dma((8,)),
            dma((8,)),
            dma,
            dma,
            dma((3, 3)),
            dma((3, 3)),
            dma((5,)),
        ]
        + ATTENTION_SCRATCH,
        compiler_params=pltpu.CompilerParams(collective_id=0, has_side_effects=True, vmem_limit_bytes=60 * MIB),
    )(
        gu, ex, key_rows, value_rows, queries, out_grad, xt, gt, ids, probs,
        jnp.asarray(UNFOLD, bf16), jnp.asarray(FOLDING, bf16),
    )


def unfold_matrix():
    out = np.zeros((3 * 80, 256), np.float32)
    for p in range(16):
        for k in range(3):
            for s in range(CAP):
                out[k * 80 + p * CAP + s, p * 16 + k * CAP + s] = 1
    return out


UNFOLD = unfold_matrix()
FOLDING = UNFOLD.reshape(3, 80, 256).transpose(0, 2, 1)


def per_device(queries, key_rows, value_rows, out_grad, tokens, token_grad, route_ids, route_probs, entry_weight, exit_weight):
    hidden = exit_weight.shape[1]
    query_grad, key_grad, value_grad, input_grad, entry_grad, exit_grad = layer_call(
        entry_weight[0].transpose(1, 2, 0), exit_weight[0], key_rows[0], value_rows[0], queries[0], out_grad[0],
        tokens[0].T, token_grad[0].T, route_ids[0].T, route_probs[0].T, hidden,
    )
    return (
        query_grad[None],
        key_grad[None],
        value_grad[None],
        input_grad.T[None],
        entry_grad.transpose(2, 0, 1)[None],
        exit_grad[None],
    )


def solution(mesh):
    row = P("exp", "ctx", None)
    entry = P("exp", None, None, "ctx")
    return jax.shard_map(
        per_device,
        mesh=mesh,
        in_specs=(row,) * 8 + (entry, row),
        out_specs=(row,) * 4 + (entry, row),
        check_vma=False,
    )
```
